256 devices in a mesh: dp: 64 (over y, x, z_hi), tensor: 4 (over z_lo, core).
Axes of the slice: x: 4, y: 4, z: 8 (z_hi: 4, z_lo: 2; z = z_hi * 2 + z_lo), core: 2. Of those that a mesh axis runs over, the one named last changes fastest.
Arguments:
- layer_inputs: bfloat16 [32768, 4096], P('dp', 'tensor'), may hold values from -6 to 6
- gate_pre: bfloat16 [32768, 14336], P('dp', 'tensor'), may hold values from -6 to 6
- up_pre: bfloat16 [32768, 14336], P('dp', 'tensor'), may hold values from -6 to 6
- hidden_grad: bfloat16 [32768, 14336], P('dp', 'tensor'), may hold values from -6 to 6
- output_grad: bfloat16 [32768, 4096], P('dp', 'tensor'), may hold values from -6 to 6
- proj_in: bfloat16 [4096, 64], replicated, may hold values from -0.09375 to 0.09375
- proj_out: bfloat16 [4096, 64], replicated, may hold values from -0.09375 to 0.09375
- proj_gate: bfloat16 [14336, 64], P('tensor'), may hold values from -0.046875 to 0.046875
- proj_up: bfloat16 [14336, 64], P('tensor'), may hold values from -0.046875 to 0.046875
- proj_hidden: bfloat16 [14336, 64], P('tensor'), may hold values from -0.046875 to 0.046875
- query_grads: bfloat16 [128, 3, 64, 64], P('dp'), may hold values from -6 to 6
Outputs:
- scores: float32 [128, 64], P(None, 'dp')
The draws below stay inside these ranges and needn't reach their ends.
All inputs are finite; a program needn't handle non-finite values.
Results may differ from the reference program's by a relative error of at most 0.0053.
Values may be sent and summed in bfloat16 or wider, within the bound.
No kernel may reach another device: no remote copies, remote signals or barrier semaphores. Data moves between devices by JAX's collectives and lax.ppermute only.
A program may use at most 128 MiB of HBM per device.

```python
import jax
import jax.numpy as jnp
from jax import lax

D = 4096
FF = 14336
RANK = 64
TOK_DEV = 512
TOKENS = 32768
EXAMPLES = 64
QUERIES = 128


def level_of(own_key, extent, pieces, least, top_value):
    factor_of, own = 1.0, jax.random.fold_in(own_key, 6)
    for axis_at, blocks in pieces:
        steps = jnp.exp(jax.random.uniform(jax.random.fold_in(own, axis_at), (blocks,), jnp.float32, least / len(pieces), top_value / len(pieces)))
        factor_of = factor_of * jnp.repeat(steps, extent[axis_at] // blocks).reshape([-1 if axis == axis_at else 1 for axis in range(len(extent))])
    return factor_of


def gaussian(rng, shape, deviation, most, shards=(), kind=jnp.bfloat16):
    factor_of = level_of(rng, shape, shards, -0.22, 0.18) if shards else 1.0
    values = jax.random.normal(rng, shape, jnp.float32) * deviation * factor_of
    return jnp.minimum(jnp.maximum(values, -most), most).astype(kind)


def setup_inputs(seed: int = 0) -> dict:
    streams_of = jax.random.split(jax.random.key(seed), 12)
    return {
        "layer_inputs": gaussian(streams_of[0], (TOKENS, D), 1.0, 6.0, ((0, 64), (1, 4))),
        "gate_pre": gaussian(streams_of[1], (TOKENS, FF), 1.0, 6.0, ((0, 64), (1, 4))),
        "up_pre": gaussian(streams_of[2], (TOKENS, FF), 1.0, 6.0, ((0, 64), (1, 4))),
        "hidden_grad": gaussian(streams_of[3], (TOKENS, FF), 1.0, 6.0, ((0, 64), (1, 4))),
        "output_grad": gaussian(streams_of[4], (TOKENS, D), 1.0, 6.0, ((0, 64), (1, 4))),
        "proj_in": gaussian(streams_of[5], (D, RANK), D ** -0.5, 0.09375),
        "proj_out": gaussian(streams_of[6], (D, RANK), D ** -0.5, 0.09375),
        "proj_gate": gaussian(streams_of[7], (FF, RANK), FF ** -0.5, 0.046875, ((0, 4),)),
        "proj_up": gaussian(streams_of[8], (FF, RANK), FF ** -0.5, 0.046875, ((0, 4),)),
        "proj_hidden": gaussian(streams_of[9], (FF, RANK), FF ** -0.5, 0.046875, ((0, 4),)),
        "query_grads": gaussian(streams_of[10], (QUERIES, 3, RANK, RANK), 1.0, 6.0, ((0, 64),)),
    }


HIGH = lax.Precision.HIGHEST
DAMP = 0.1

def invert_factor(vectors, count):
    mean = jnp.dot(vectors.T.astype(jnp.float32), vectors.astype(jnp.float32), precision=HIGH, preferred_element_type=jnp.float32) / count
    eye = jnp.eye(mean.shape[0], dtype=jnp.float32)
    lower = jnp.linalg.cholesky(mean + DAMP * eye)
    return jax.scipy.linalg.cho_solve((lower, True), eye)

def project_block(args):
    inputs_b, gate_b, up_b, grad_b, outg_b, proj_in, proj_out, proj_gate, proj_up, proj_hidden = args
    gate_vals = gate_b.astype(jnp.float32)
    up_vals = up_b.astype(jnp.float32)
    grad_vals = grad_b.astype(jnp.float32)
    sigmoid_g = jax.nn.sigmoid(gate_vals)
    hidden = (gate_vals * sigmoid_g * up_vals).astype(jnp.bfloat16)
    gate_grad = (grad_vals * up_vals * sigmoid_g * (1.0 + gate_vals * (1.0 - sigmoid_g))).astype(jnp.bfloat16)
    up_grad = (grad_vals * gate_vals * sigmoid_g).astype(jnp.bfloat16)
    return (jnp.dot(inputs_b.astype(jnp.float32), proj_in.astype(jnp.float32), preferred_element_type=jnp.float32), jnp.dot(gate_grad.astype(jnp.float32), proj_gate.astype(jnp.float32), preferred_element_type=jnp.float32), jnp.dot(up_grad.astype(jnp.float32), proj_up.astype(jnp.float32), preferred_element_type=jnp.float32), jnp.dot(hidden.astype(jnp.float32), proj_hidden.astype(jnp.float32), preferred_element_type=jnp.float32), jnp.dot(outg_b.astype(jnp.float32), proj_out.astype(jnp.float32), preferred_element_type=jnp.float32))

def reference(layer_inputs, gate_pre, up_pre, hidden_grad, output_grad, proj_in, proj_out, proj_gate, proj_up, proj_hidden, query_grads):
    blocks = TOKENS // TOK_DEV

    def split_rows(array):
        return array.reshape(blocks, TOK_DEV, array.shape[1])

    def one_block(items):
        return project_block(items + (proj_in, proj_out, proj_gate, proj_up, proj_hidden))
    stacked = lax.map(one_block, (split_rows(layer_inputs), split_rows(gate_pre), split_rows(up_pre), split_rows(hidden_grad), split_rows(output_grad)))
    in_proj, gate_proj, up_proj, hid_proj, out_proj = [v.reshape(TOKENS, RANK) for v in stacked]
    inv_in = invert_factor(in_proj, TOKENS)
    inv_gate = invert_factor(gate_proj, TOKENS)
    inv_up = invert_factor(up_proj, TOKENS)
    inv_hid = invert_factor(hid_proj, TOKENS)
    inv_out = invert_factor(out_proj, TOKENS)

    def per_example(out_vals, in_vals):
        out_blocks = out_vals.reshape(EXAMPLES, TOK_DEV, RANK)
        in_blocks = in_vals.reshape(EXAMPLES, TOK_DEV, RANK)
        summed = jnp.einsum('bto,bti->boi', out_blocks, in_blocks, precision=HIGH)
        return summed.reshape(EXAMPLES, RANK * RANK)
    train_grads = jnp.concatenate([per_example(gate_proj, in_proj), per_example(up_proj, in_proj), per_example(out_proj, hid_proj)], axis=1).astype(jnp.bfloat16)
    left_inv = jnp.stack([inv_gate, inv_up, inv_out])
    right_inv = jnp.stack([inv_in, inv_in, inv_hid])
    queries = query_grads.astype(jnp.float32)
    precond = jnp.einsum('loa,qlab,lbi->qloi', left_inv, queries, right_inv, precision=HIGH)
    precond = precond.reshape(QUERIES, 3 * RANK * RANK).astype(jnp.bfloat16)
    factor = 1.0 / (RANK * RANK)
    return jnp.dot(precond.astype(jnp.float32), train_grads.T.astype(jnp.float32), preferred_element_type=jnp.float32) * factor
```

```python
import jax
import jax.numpy as jnp
from jax import lax
from jax.experimental import pallas as pl
from jax.experimental.pallas import tpu as pltpu
from jax.sharding import PartitionSpec as P

HIGH = lax.Precision.HIGHEST
DAMP = 0.1
RANK = 64
WIDE = 2 * RANK
CHUNK = 512
STRIP = 128
SIDE = 4
VMEM_BYTES = 48 * 1024 * 1024

RINGS = {"y": 16, "x": 4, "z": 1}


def layer_of(tensor_at):
    return lax.rem(tensor_at, 3)


def project_kernel(
    gate_hbm, up_hbm, grad_hbm, inputs_hbm, outg_hbm,
    win_hbm, wout_hbm, wgate_hbm, wup_hbm, whid_hbm, query_ref,
    own_ref, next_ref, across_ref, last_ref, pieces_ref,
    gate_buf, up_buf, grad_buf, inputs_buf, outg_buf,
    win_buf, wout_buf, wgate_buf, wup_buf, whid_buf,
    sum_gate, sum_up, sum_down, hid_s, gg_s, ug_s, sems, side_sems,
):
    tensor_at = lax.axis_index("tensor")
    tokens, hidden = gate_hbm.shape
    features = inputs_hbm.shape[1]
    chunks = hidden // CHUNK

    def side_copies():
        mine = pl.ds(pl.multiple_of(tensor_at * features, features), features)
        return (
            pltpu.make_async_copy(inputs_hbm, inputs_buf, side_sems.at[0]),
            pltpu.make_async_copy(win_hbm.at[mine, :], win_buf, side_sems.at[1]),
            pltpu.make_async_copy(outg_hbm, outg_buf, side_sems.at[2]),
            pltpu.make_async_copy(wout_hbm.at[mine, :], wout_buf, side_sems.at[3]),
        )

    def chunk_copies(c):
        at = pl.ds(pl.multiple_of(c * CHUNK, CHUNK), CHUNK)
        wide = [(gate_hbm, gate_buf), (up_hbm, up_buf), (grad_hbm, grad_buf)]
        tall = [(wgate_hbm, wgate_buf), (wup_hbm, wup_buf), (whid_hbm, whid_buf)]
        return [
            pltpu.make_async_copy(src.at[:, at], dst.at[c], sems.at[c, i])
            for i, (src, dst) in enumerate(wide)
        ] + [
            pltpu.make_async_copy(src.at[at, :], dst.at[c], sems.at[c, 3 + i])
            for i, (src, dst) in enumerate(tall)
        ]

    for c in side_copies():
        c.start()
    for c in range(chunks):
        for copy in chunk_copies(c):
            copy.start()

    layer = layer_of(tensor_at)
    for q in range(2):
        rows = query_ref[q, layer].astype(jnp.float32)
        rows = jnp.where(layer == 2, rows.T, rows)
        packed = jnp.concatenate([rows[: RANK // 2], rows[RANK // 2 :]], axis=1)
        pieces_ref[q * (RANK // 2) : (q + 1) * (RANK // 2), :] = packed.astype(jnp.bfloat16)

    for copy in side_copies():
        copy.wait()
    zeros = jnp.zeros((features, RANK), jnp.bfloat16)
    right_in = jnp.concatenate([zeros, win_buf[...]], axis=1)
    right_out = jnp.concatenate([zeros, wout_buf[...]], axis=1)
    part_in = jnp.dot(inputs_buf[...], right_in, preferred_element_type=jnp.float32)
    sum_gate[...] = part_in
    sum_up[...] = part_in
    sum_down[...] = jnp.dot(outg_buf[...], right_out, preferred_element_type=jnp.float32)

    @pl.loop(0, chunks)
    def _(c):
        for copy in chunk_copies(c):
            copy.wait()
        pad = jnp.zeros((CHUNK, RANK), jnp.bfloat16)
        for r in range(tokens // STRIP):
            at = slice(r * STRIP, (r + 1) * STRIP)
            g = gate_buf[c, at, :].astype(jnp.float32)
            u = up_buf[c, at, :].astype(jnp.float32)
            e = grad_buf[c, at, :].astype(jnp.float32)
            s = 0.5 * jnp.tanh(0.5 * g) + 0.5
            a = g * s
            hid_s[at, :] = (a * u).astype(jnp.bfloat16)
            ug_s[at, :] = (e * a).astype(jnp.bfloat16)
            gg_s[at, :] = (e * u * (s + a * (1.0 - s))).astype(jnp.bfloat16)
        for acc, val, w in ((sum_gate, gg_s, wgate_buf), (sum_up, ug_s, wup_buf), (sum_down, hid_s, whid_buf)):
            left = jnp.concatenate([w[c], pad], axis=1)
            acc[...] += jnp.dot(val[...], left, preferred_element_type=jnp.float32)

    sums = (sum_gate, sum_up, sum_down, sum_gate)
    outs = (own_ref, next_ref, across_ref, last_ref)
    for t in range(4):
        @pl.when(tensor_at == t)
        def _():
            for s in range(4):
                outs[s][...] = sums[(t + s) % 4][...].astype(jnp.bfloat16)


def project(gate_pre, up_pre, hidden_grad, layer_inputs, output_grad, proj_in, proj_out, proj_gate, proj_up, proj_hidden, query_grads):
    tokens, hidden = gate_pre.shape
    features = layer_inputs.shape[1]
    chunks = hidden // CHUNK
    half = jax.ShapeDtypeStruct((tokens, WIDE), jnp.bfloat16)
    anywhere = pl.BlockSpec(memory_space=pl.ANY)
    inside = pl.BlockSpec(memory_space=pltpu.VMEM)
    buf = lambda *shape: pltpu.VMEM(shape, jnp.bfloat16)
    flops = 2 * tokens * (3 * hidden + 2 * features) * RANK
    return pl.pallas_call(
        project_kernel,
        out_shape=[half] * 4 + [jax.ShapeDtypeStruct((RANK, WIDE), jnp.bfloat16)],
        in_specs=[anywhere] * 10 + [inside],
        out_specs=[inside] * 5,
        scratch_shapes=[
            buf(chunks, tokens, CHUNK), buf(chunks, tokens, CHUNK), buf(chunks, tokens, CHUNK),
            buf(tokens, features), buf(tokens, features),
            buf(features, RANK), buf(features, RANK),
            buf(chunks, CHUNK, RANK), buf(chunks, CHUNK, RANK), buf(chunks, CHUNK, RANK),
            pltpu.VMEM((tokens, WIDE), jnp.float32), pltpu.VMEM((tokens, WIDE), jnp.float32), pltpu.VMEM((tokens, WIDE), jnp.float32),
            buf(tokens, CHUNK), buf(tokens, CHUNK), buf(tokens, CHUNK),
            pltpu.SemaphoreType.DMA((chunks, 6)),
            pltpu.SemaphoreType.DMA((4,)),
        ],
        compiler_params=pltpu.CompilerParams(vmem_limit_bytes=VMEM_BYTES),
        cost_estimate=pl.CostEstimate(flops=flops, bytes_accessed=17_000_000, transcendentals=tokens * hidden),
        name="project",
    )(gate_pre, up_pre, hidden_grad, layer_inputs, output_grad, proj_in, proj_out, proj_gate, proj_up, proj_hidden, query_grads)


def gram_kernel(own_ref, a_ref, b_ref, c_ref, factor_ref, cross_ref):
    f32 = jnp.float32
    v = (own_ref[...].astype(f32) + a_ref[...].astype(f32)) + (b_ref[...].astype(f32) + c_ref[...].astype(f32))
    m = lax.dot_general(v, v, (((0,), (0,)), ((), ())), precision=HIGH, preferred_element_type=f32)
    left = lax.broadcasted_iota(jnp.int32, (RANK, WIDE), 1) < RANK
    factor_ref[...] = jnp.where(left, m[:RANK], m[RANK:])
    cross_ref[...] = jnp.where(left, m[RANK:], m[:RANK])


def gram(parts):
    inside = pl.BlockSpec(memory_space=pltpu.VMEM)
    pair = jax.ShapeDtypeStruct((RANK, WIDE), jnp.float32)
    return pl.pallas_call(
        gram_kernel,
        out_shape=[pair, pair],
        in_specs=[inside] * 4,
        out_specs=[inside] * 2,
        name="gram",
    )(*parts)


def invert_pair(w):
    lane = lax.broadcasted_iota(jnp.int32, (RANK, WIDE), 1)
    row_at = lax.broadcasted_iota(jnp.int32, (RANK, WIDE), 0)
    left = lane < RANK
    column_at = jnp.where(left, lane, lane - RANK)
    for k in range(RANK):
        col = jnp.where(
            left,
            jnp.broadcast_to(w[:, k : k + 1], (RANK, WIDE)),
            jnp.broadcast_to(w[:, RANK + k : RANK + k + 1], (RANK, WIDE)),
        )
        here = column_at == k
        inv = 1.0 / col[k : k + 1, :]
        row = jnp.where(here[k : k + 1, :], 1.0, w[k : k + 1, :]) * inv
        w = jnp.where(row_at == k, row, jnp.where(here, 0.0, w) - col * row)
    return w


def score_kernel(count, factor_ref, cross_ref, q0_ref, q1_ref, q2_ref, q3_ref, out_ref):
    f32 = jnp.float32
    lane = lax.broadcasted_iota(jnp.int32, (RANK, WIDE), 1)
    row_at = lax.broadcasted_iota(jnp.int32, (RANK, WIDE), 0)
    diag = (lane == row_at) | (lane == row_at + RANK)
    inv = invert_pair(factor_ref[...] * (1.0 / count) + jnp.where(diag, DAMP, 0.0))
    dot = lambda a, b: jnp.dot(a, b, precision=HIGH, preferred_element_type=f32)
    h = dot(dot(inv[:, :RANK], cross_ref[:, RANK:]), inv[:, RANK:])
    h = jnp.concatenate([h[: RANK // 2], h[RANK // 2 :]], axis=1).reshape(1, SIDE, 8, WIDE)
    sums = []
    for ref in (q0_ref, q1_ref, q2_ref, q3_ref):
        q = ref[...].astype(f32).reshape(ref.shape[0] // (RANK // 2), SIDE, 8, WIDE)
        sums.append((q * h).sum(axis=1).reshape(ref.shape[0] // SIDE, WIDE))
    sums = jnp.concatenate(sums, axis=0)
    queries = sums.shape[0] // 8
    me = lax.axis_index("dp")
    j = lax.shift_right_logical(lax.broadcasted_iota(jnp.int32, (queries, sums.shape[0]), 1), 3)
    want = lax.broadcasted_iota(jnp.int32, (queries, sums.shape[0]), 0)
    y = (lax.shift_right_logical(me, 4) - lax.shift_right_logical(j, 5)) & 3
    x = (lax.shift_right_logical(me, 2) - lax.shift_right_logical(j, 3)) & 3
    z = (me - lax.shift_right_logical(j, 1)) & 3
    source = y * 32 + x * 8 + z * 2 + (j & 1)
    place = jnp.where(source == want, 1.0, 0.0).astype(f32)
    by_query = dot(place, sums)
    ones = jnp.full((8, WIDE), 1.0 / (RANK * RANK), f32)
    row = lax.dot_general(ones, by_query, (((1,), (1,)), ((), ())), precision=HIGH, preferred_element_type=f32)
    out_ref[...] = jnp.where(lax.axis_index("tensor") == 3, 0.0, row[:1])


def score(count, factor, cross, queries):
    inside = pl.BlockSpec(memory_space=pltpu.VMEM)
    total = sum(q.shape[0] for q in queries) // (RANK // 2)
    return pl.pallas_call(
        lambda *refs: score_kernel(count, *refs),
        out_shape=jax.ShapeDtypeStruct((1, total), jnp.float32),
        in_specs=[inside] * 6,
        out_specs=inside,
        compiler_params=pltpu.CompilerParams(vmem_limit_bytes=VMEM_BYTES),
        name="score",
    )(factor, cross, *queries)


def ring(stride, step, size):
    def to(i):
        at = (i // stride) % SIDE
        return i + ((at + step) % SIDE - at) * stride

    return [(i, to(i)) for i in range(size)]


def body(
    layer_inputs, gate_pre, up_pre, hidden_grad, output_grad,
    proj_in, proj_out, proj_gate, proj_up, proj_hidden, query_grads,
):
    size = lax.axis_size("dp")

    def around(value, name):
        return [value] + [lax.ppermute(value, "dp", ring(RINGS[name], s, size)) for s in (1, 2, 3)]

    def total(parts):
        return (parts[0] + parts[1]) + (parts[2] + parts[3])

    def shifted(value, step):
        return lax.ppermute(value, "tensor", [(i, (i + step) % 4) for i in range(4)])

    own, nxt, across, last, pieces = project(
        gate_pre, up_pre, hidden_grad, layer_inputs, output_grad,
        proj_in, proj_out, proj_gate, proj_up, proj_hidden, query_grads,
    )
    factor, cross = gram((own, shifted(nxt, 1), shifted(across, 2), shifted(last, 3)))
    pieces = jnp.concatenate(around(pieces, "z"), axis=0)
    factor = total(around(factor, "y"))
    pieces = jnp.concatenate(around(pieces, "x"), axis=0)
    factor = total(around(factor, "x"))
    queries = around(pieces, "y")
    factor = total(around(factor, "z"))
    count = layer_inputs.shape[0] * size
    part = score(count, factor, cross, queries)
    parts = [part] + [shifted(part, s) for s in (1, 2, 3)]
    at = lax.axis_index("tensor")

    def of(index):
        picked = parts[3]
        for s in (2, 1, 0):
            picked = jnp.where((at - index) % 4 == s, parts[s], picked)
        return picked

    return ((of(0) + of(1)) + of(2)).reshape(-1, 1)


def solution(mesh):
    placed = (
        P("dp", "tensor"), P("dp", "tensor"), P("dp", "tensor"), P("dp", "tensor"), P("dp", "tensor"),
        P(), P(), P("tensor", None), P("tensor", None), P("tensor", None),
        P("dp", None, None, None),
    )
    return jax.shard_map(body, mesh=mesh, in_specs=placed, out_specs=P(None, "dp"), check_vma=False)
```

```python
import jax
import jax.numpy as jnp
from jax import lax
from jax.experimental import pallas as pl
from jax.experimental.pallas import tpu as pltpu
from jax.sharding import PartitionSpec as P

HIGH = lax.Precision.HIGHEST
DAMP = 0.1
RANK = 64
WIDE = 2 * RANK
CHUNK = 512
STRIP = 64
AHEAD = 3
SIDE = 4
VMEM_BYTES = 60 * 1024 * 1024

TERMS = 3
FACTOR_ROWS = TERMS * RANK
SMALL_VMEM = 32 * 1024 * 1024
RINGS = {"y": 16, "x": 4, "z": 1}


def layer_of(tensor_at):
    return lax.rem(tensor_at, 3)


def rows_dot(a, b):
    return lax.dot_general(a, b, (((1,), (1,)), ((), ())), preferred_element_type=jnp.float32)


def project_kernel(
    gate_hbm, up_hbm, grad_hbm, inputs_hbm, outg_hbm,
    win_hbm, wout_hbm, wgate_hbm, wup_hbm, whid_hbm, query_hbm,
    own_ref, next_ref, across_ref, last_ref, pieces_ref,
    hidden_buf, side_buf, hidden_w, side_w, query_buf, acts, sums, sems, side_sems,
):
    tensor_at = lax.axis_index("tensor")
    tokens, hidden = gate_hbm.shape
    features = inputs_hbm.shape[1]
    chunks = hidden // CHUNK

    def side_copies():
        mine = pl.ds(pl.multiple_of(tensor_at * features, features), features)
        return [
            pltpu.make_async_copy(src, side_buf.at[i], side_sems.at[i])
            for i, src in enumerate((inputs_hbm, outg_hbm))
        ] + [
            pltpu.make_async_copy(src.at[:, mine], side_w.at[i, RANK:, :], side_sems.at[2 + i])
            for i, src in enumerate((win_hbm, wout_hbm))
        ]

    def weight_copies():
        return [
            pltpu.make_async_copy(src, hidden_w.at[i, :RANK, :], side_sems.at[5 + i])
            for i, src in enumerate((wgate_hbm, wup_hbm, whid_hbm))
        ]

    def chunk_copies(c):
        at = pl.ds(pl.multiple_of(c * CHUNK, CHUNK), CHUNK)
        return [
            pltpu.make_async_copy(src.at[:, at], hidden_buf.at[i, c], sems.at[i, c])
            for i, src in enumerate((gate_hbm, up_hbm, grad_hbm))
        ]

    def start(copies):
        for copy in copies:
            copy.start()

    def arrive(copies):
        for copy in copies:
            copy.wait()

    query_copy = pltpu.make_async_copy(query_hbm, query_buf, side_sems.at[4])
    query_copy.start()
    for c in range(AHEAD):
        start(chunk_copies(c))

    hidden_w[:, RANK:, :] = jnp.zeros_like(hidden_w[:, RANK:, :])
    side_w[:, :RANK, :] = jnp.zeros_like(side_w[:, :RANK, :])

    query_copy.wait()
    layer = layer_of(tensor_at)
    for q in range(2):
        rows = query_buf[q, layer].astype(jnp.float32)
        rows = jnp.where(layer == 2, rows.T, rows)
        packed = jnp.concatenate([rows[: RANK // 2], rows[RANK // 2 :]], axis=1)
        pieces_ref[q * (RANK // 2) : (q + 1) * (RANK // 2), :] = packed.astype(jnp.bfloat16)

    @pl.loop(0, chunks)
    def _(c):
        arrive(chunk_copies(c))

        @pl.when(c + AHEAD < chunks)
        def _():
            start(chunk_copies(c + AHEAD))

        @pl.when(c == 0)
        def _():
            start(weight_copies())

        @pl.when(c == 1)
        def _():
            start(side_copies())

        columns = pl.ds(pl.multiple_of(c * CHUNK, CHUNK), CHUNK)

        @pl.loop(0, tokens // STRIP)
        def _(r):
            at = pl.ds(pl.multiple_of(r * STRIP, STRIP), STRIP)
            half = 0.5 * hidden_buf[0, c, at, :].astype(jnp.float32)
            u = hidden_buf[1, c, at, :].astype(jnp.float32)
            e = hidden_buf[2, c, at, :].astype(jnp.float32)
            th = jnp.tanh(half)
            p = 1.0 + th
            a = half * p
            acts[0, at, columns] = (0.5 * (e * u) * (p + a * (1.0 - th))).astype(jnp.bfloat16)
            acts[1, at, columns] = (e * a).astype(jnp.bfloat16)
            acts[2, at, columns] = (a * u).astype(jnp.bfloat16)

    arrive(weight_copies())

    @pl.loop(0, 3)
    def _(i):
        sums[i] = rows_dot(acts[i], hidden_w[i])

    arrive(side_copies())

    @pl.loop(0, 2)
    def _(i):
        sums[2 * i] += rows_dot(side_buf[i], side_w[i])

    right = lax.broadcasted_iota(jnp.int32, (tokens, WIDE), 1) >= RANK
    sums[1] = jnp.where(right, sums[0], sums[1])
    for s, out in enumerate((own_ref, next_ref, across_ref, last_ref)):
        out[...] = sums[layer_of(lax.rem(tensor_at + s, 4))].astype(jnp.bfloat16)


def project(gate_pre, up_pre, hidden_grad, layer_inputs, output_grad, proj_in, proj_out, proj_gate, proj_up, proj_hidden, query_grads):
    tokens, hidden = gate_pre.shape
    features = layer_inputs.shape[1]
    chunks = hidden // CHUNK
    half = jax.ShapeDtypeStruct((tokens, WIDE), jnp.bfloat16)
    inside = pl.BlockSpec(memory_space=pltpu.VMEM)
    buf = lambda *shape: pltpu.VMEM(shape, jnp.bfloat16)
    flops = 2 * tokens * (3 * hidden + 2 * features) * RANK
    return pl.pallas_call(
        project_kernel,
        out_shape=[half] * 4 + [jax.ShapeDtypeStruct((RANK, WIDE), jnp.bfloat16)],
        in_specs=[pl.BlockSpec(memory_space=pltpu.HBM)] * 11,
        out_specs=[inside] * 5,
        scratch_shapes=[
            buf(3, chunks, tokens, CHUNK),
            buf(2, tokens, features),
            buf(3, WIDE, hidden),
            buf(2, WIDE, features),
            buf(*query_grads.shape),
            buf(3, tokens, hidden),
            pltpu.VMEM((3, tokens, WIDE), jnp.float32),
            pltpu.SemaphoreType.DMA((3, chunks)),
            pltpu.SemaphoreType.DMA((8,)),
        ],
        compiler_params=pltpu.CompilerParams(vmem_limit_bytes=VMEM_BYTES),
        cost_estimate=pl.CostEstimate(flops=flops, bytes_accessed=17_000_000, transcendentals=tokens * hidden),
        name="project",
    )(gate_pre, up_pre, hidden_grad, layer_inputs, output_grad, proj_in.T, proj_out.T, proj_gate.T, proj_up.T, proj_hidden.T, query_grads)


def put_sum(out_ref, value):
    for i in range(TERMS):
        term = value.astype(jnp.bfloat16)
        out_ref[i * RANK : (i + 1) * RANK, :] = term
        value = value - term.astype(jnp.float32)


def get_sum(ref):
    terms = [ref[i * RANK : (i + 1) * RANK, :].astype(jnp.float32) for i in range(TERMS)]
    return (terms[2] + terms[1]) + terms[0]


def total_of(refs):
    parts = [get_sum(ref) for ref in refs]
    return (parts[0] + parts[1]) + (parts[2] + parts[3])


def gram_kernel(own_ref, a_ref, b_ref, c_ref, pieces_ref, message_ref, cross_ref):
    f32 = jnp.float32
    v = (own_ref[...].astype(f32) + a_ref[...].astype(f32)) + (b_ref[...].astype(f32) + c_ref[...].astype(f32))
    m = lax.dot_general(v, v, (((0,), (0,)), ((), ())), precision=HIGH, preferred_element_type=f32)
    left = lax.broadcasted_iota(jnp.int32, (RANK, WIDE), 1) < RANK
    put_sum(message_ref, jnp.where(left, m[:RANK], m[RANK:]))
    message_ref[FACTOR_ROWS:, :] = pieces_ref[...]
    cross_ref[...] = jnp.where(left, m[RANK:], m[:RANK])


def gram(parts, pieces):
    inside = pl.BlockSpec(memory_space=pltpu.VMEM)
    return pl.pallas_call(
        gram_kernel,
        out_shape=[
            jax.ShapeDtypeStruct((FACTOR_ROWS + pieces.shape[0], WIDE), jnp.bfloat16),
            jax.ShapeDtypeStruct((RANK, WIDE), jnp.float32),
        ],
        in_specs=[inside] * 5,
        out_specs=[inside] * 2,
        compiler_params=pltpu.CompilerParams(vmem_limit_bytes=SMALL_VMEM),
        name="gram",
    )(*parts, pieces)


def merge_kernel(*refs):
    parts, out_ref = refs[:-1], refs[-1]
    put_sum(out_ref, total_of(parts))
    rows = parts[0].shape[0] - FACTOR_ROWS
    for i, ref in enumerate(parts):
        out_ref[FACTOR_ROWS + i * rows : FACTOR_ROWS + (i + 1) * rows, :] = ref[FACTOR_ROWS:, :]


def merge(parts):
    inside = pl.BlockSpec(memory_space=pltpu.VMEM)
    rows = FACTOR_ROWS + SIDE * (parts[0].shape[0] - FACTOR_ROWS)
    return pl.pallas_call(
        merge_kernel,
        out_shape=jax.ShapeDtypeStruct((rows, WIDE), jnp.bfloat16),
        in_specs=[inside] * SIDE,
        out_specs=inside,
        compiler_params=pltpu.CompilerParams(vmem_limit_bytes=SMALL_VMEM),
        name="merge",
    )(*parts)


def invert_pair(w):
    lane = lax.broadcasted_iota(jnp.int32, (RANK, WIDE), 1)
    row_at = lax.broadcasted_iota(jnp.int32, (RANK, WIDE), 0)
    left = lane < RANK
    column_at = jnp.where(left, lane, lane - RANK)
    for k in range(RANK):
        col = jnp.where(
            left,
            jnp.broadcast_to(w[:, k : k + 1], (RANK, WIDE)),
            jnp.broadcast_to(w[:, RANK + k : RANK + k + 1], (RANK, WIDE)),
        )
        here = column_at == k
        inv = 1.0 / col[k : k + 1, :]
        row = jnp.where(here[k : k + 1, :], 1.0, w[k : k + 1, :]) * inv
        w = jnp.where(row_at == k, row, jnp.where(here, 0.0, w) - col * row)
    return w


def score_kernel(count, cross_ref, *refs):
    parts, out_ref = refs[:-1], refs[-1]
    f32 = jnp.float32
    lane = lax.broadcasted_iota(jnp.int32, (RANK, WIDE), 1)
    row_at = lax.broadcasted_iota(jnp.int32, (RANK, WIDE), 0)
    diag = (lane == row_at) | (lane == row_at + RANK)
    inv = invert_pair(total_of(parts) * (1.0 / count) + jnp.where(diag, DAMP, 0.0))
    dot = lambda a, b: jnp.dot(a, b, precision=HIGH, preferred_element_type=f32)
    h = dot(dot(inv[:, :RANK], cross_ref[:, RANK:]), inv[:, RANK:])
    h = jnp.concatenate([h[: RANK // 2], h[RANK // 2 :]], axis=1).reshape(1, SIDE, 8, WIDE)
    sums = []
    for ref in parts:
        q = ref[FACTOR_ROWS:, :].astype(f32)
        q = q.reshape(q.shape[0] // (RANK // 2), SIDE, 8, WIDE)
        sums.append((q * h).sum(axis=1).reshape(q.shape[0] * 8, WIDE))
    sums = jnp.concatenate(sums, axis=0)
    queries = sums.shape[0] // 8
    me = lax.axis_index("dp")
    j = lax.shift_right_logical(lax.broadcasted_iota(jnp.int32, (queries, sums.shape[0]), 1), 3)
    want = lax.broadcasted_iota(jnp.int32, (queries, sums.shape[0]), 0)
    last, middle = lax.shift_right_logical(j, 5), lax.shift_right_logical(j, 3)
    swap = (lax.axis_index("tensor") & 1) == 1
    y = (lax.shift_right_logical(me, 4) - jnp.where(swap, middle, last)) & 3
    x = (lax.shift_right_logical(me, 2) - jnp.where(swap, last, middle)) & 3
    z = (me - lax.shift_right_logical(j, 1)) & 3
    source = y * 32 + x * 8 + z * 2 + (j & 1)
    place = jnp.where(source == want, 1.0, 0.0).astype(f32)
    by_query = dot(place, sums)
    ones = jnp.full((8, WIDE), 1.0 / (RANK * RANK), f32)
    row = lax.dot_general(ones, by_query, (((1,), (1,)), ((), ())), precision=HIGH, preferred_element_type=f32)
    out_ref[...] = jnp.where(lax.axis_index("tensor") == 3, 0.0, row[:1])


def score(count, cross, parts):
    inside = pl.BlockSpec(memory_space=pltpu.VMEM)
    total = sum(p.shape[0] - FACTOR_ROWS for p in parts) // (RANK // 2)
    return pl.pallas_call(
        lambda *refs: score_kernel(count, *refs),
        out_shape=jax.ShapeDtypeStruct((1, total), jnp.float32),
        in_specs=[inside] * (1 + SIDE),
        out_specs=inside,
        compiler_params=pltpu.CompilerParams(vmem_limit_bytes=SMALL_VMEM),
        name="score",
    )(cross, *parts)


def ring(names, step, size):
    def to(i, t):
        stride = RINGS[names[t & 1]]
        at = (i // stride) % SIDE
        return (i + ((at + step) % SIDE - at) * stride) * 4 + t

    return [(i * 4 + t, to(i, t)) for i in range(size) for t in range(4)]


def body(
    layer_inputs, gate_pre, up_pre, hidden_grad, output_grad,
    proj_in, proj_out, proj_gate, proj_up, proj_hidden, query_grads,
):
    size = lax.axis_size("dp")

    def around(value, names):
        far, near, back = [lax.ppermute(value, ("dp", "tensor"), ring(names, s, size)) for s in (2, 1, 3)]
        return [value, near, far, back]

    def shifted(value, step):
        return lax.ppermute(value, "tensor", [(i, (i + step) % 4) for i in range(4)])

    own, nxt, across, last, pieces = project(
        gate_pre, up_pre, hidden_grad, layer_inputs, output_grad,
        proj_in, proj_out, proj_gate, proj_up, proj_hidden, query_grads,
    )
    message, cross = gram((own, shifted(nxt, 1), shifted(across, 2), shifted(last, 3)), pieces)
    message = merge(around(message, "zz"))
    message = merge(around(message, "xy"))
    part = score(layer_inputs.shape[0] * size, cross, around(message, "yx"))
    parts = [part] + [shifted(part, s) for s in (1, 2, 3)]
    at = lax.axis_index("tensor")

    def of(index):
        picked = parts[3]
        for s in (2, 1, 0):
            picked = jnp.where((at - index) % 4 == s, parts[s], picked)
        return picked

    return ((of(0) + of(1)) + of(2)).reshape(-1, 1)


def solution(mesh):
    placed = (
        P("dp", "tensor"), P("dp", "tensor"), P("dp", "tensor"), P("dp", "tensor"), P("dp", "tensor"),
        P(), P(), P("tensor", None), P("tensor", None), P("tensor", None),
        P("dp", None, None, None),
    )
    return jax.shard_map(body, mesh=mesh, in_specs=placed, out_specs=P(None, "dp"), check_vma=False)
```

```python
import jax
import jax.numpy as jnp
from jax import lax
from jax.experimental import pallas as pl
from jax.experimental.pallas import tpu as pltpu
from jax.sharding import PartitionSpec as P

HIGH = lax.Precision.HIGHEST
DAMP = 0.1
RANK = 64
WIDE = 2 * RANK
STRIP = 128
AHEAD = 3
SIDE = 4
VMEM_BYTES = 32 * 1024 * 1024

TERMS = 3
FACTOR_ROWS = TERMS * RANK
SMALL_VMEM = 32 * 1024 * 1024
RINGS = {"y": 16, "x": 4, "z": 1}


def layer_of(tensor_at):
    return lax.rem(tensor_at, 3)


def rows_dot(a, b):
    return lax.dot_general(a, b, (((1,), (1,)), ((), ())), preferred_element_type=jnp.float32)


def project_kernel(
    gate_hbm, up_hbm, grad_hbm, inputs_hbm, outg_hbm,
    win_hbm, wout_hbm, wgate_hbm, wup_hbm, whid_hbm, query_hbm,
    own_ref, next_ref, across_ref, last_ref, pieces_ref,
    hidden_buf, side_buf, hidden_w, side_w, query_buf, sums, sems, side_sems,
):
    tensor_at = lax.axis_index("tensor")
    tokens, hidden = gate_hbm.shape
    features = inputs_hbm.shape[1]
    strips = tokens // STRIP

    def side_copies():
        mine = pl.ds(pl.multiple_of(tensor_at * features, features), features)
        return [
            pltpu.make_async_copy(src, side_buf.at[i], side_sems.at[i])
            for i, src in enumerate((inputs_hbm, outg_hbm))
        ] + [
            pltpu.make_async_copy(src.at[:, mine], side_w.at[i], side_sems.at[2 + i])
            for i, src in enumerate((win_hbm, wout_hbm))
        ]

    def weight_copies():
        return [
            pltpu.make_async_copy(src, hidden_w.at[i], side_sems.at[5 + i])
            for i, src in enumerate((wgate_hbm, wup_hbm, whid_hbm))
        ]

    def chunk_copies(c):
        rows = pl.ds(pl.multiple_of(c * STRIP, STRIP), STRIP)
        return [
            pltpu.make_async_copy(src.at[rows, :], hidden_buf.at[i, rows, :], sems.at[i, c])
            for i, src in enumerate((gate_hbm, up_hbm, grad_hbm))
        ]

    def start(copies):
        for copy in copies:
            copy.start()

    def arrive(copies):
        for copy in copies:
            copy.wait()

    query_copy = pltpu.make_async_copy(query_hbm, query_buf, side_sems.at[4])
    query_copy.start()
    start(weight_copies())
    start(chunk_copies(0))

    @pl.loop(0, strips)
    def _(c):
        arrive(chunk_copies(c))

        @pl.when(c == 0)
        def _():
            for k in range(1, 3):
                start(chunk_copies(k))
            arrive(weight_copies())

        @pl.when((c > 0) & (c + 2 < strips))
        def _():
            start(chunk_copies(c + 2))

        @pl.when(c == 2)
        def _():
            start(side_copies())

        at = pl.ds(pl.multiple_of(c * STRIP, STRIP), STRIP)
        g = hidden_buf[0, at, :].astype(jnp.float32)
        u = hidden_buf[1, at, :].astype(jnp.float32)
        e = hidden_buf[2, at, :].astype(jnp.float32)
        th = jnp.tanh(0.5 * g)
        p, q = 1.0 + th, 1.0 - th
        a = g * p
        gate_grad = ((e * u) * (p * (2.0 + g * q))).astype(jnp.bfloat16)
        up_grad = (e * a).astype(jnp.bfloat16)
        hid = (a * u).astype(jnp.bfloat16)
        for i, act in enumerate((gate_grad, up_grad, hid)):
            sums[i, at, :RANK] = rows_dot(act, hidden_w[i]) * (0.25 if i == 0 else 0.5)

    arrive(side_copies())

    @pl.loop(0, 2)
    def _(i):
        sums[2 * i, :, RANK:] = rows_dot(side_buf[i], side_w[i])

    query_copy.wait()
    layer = layer_of(tensor_at)
    for q in range(2):
        rows = query_buf[q, layer].astype(jnp.float32)
        rows = jnp.where(layer == 2, rows.T, rows)
        packed = jnp.concatenate([rows[: RANK // 2], rows[RANK // 2 :]], axis=1)
        pieces_ref[q * (RANK // 2) : (q + 1) * (RANK // 2), :] = packed.astype(jnp.bfloat16)

    sums[1, :, RANK:] = sums[0, :, RANK:]
    for s, out in enumerate((own_ref, next_ref, across_ref, last_ref)):
        out[...] = sums[layer_of(lax.rem(tensor_at + s, 4))].astype(jnp.bfloat16)


def project(gate_pre, up_pre, hidden_grad, layer_inputs, output_grad, proj_in, proj_out, proj_gate, proj_up, proj_hidden, query_grads):
    tokens, hidden = gate_pre.shape
    features = layer_inputs.shape[1]
    half = jax.ShapeDtypeStruct((tokens, WIDE), jnp.bfloat16)
    inside = pl.BlockSpec(memory_space=pltpu.VMEM)
    buf = lambda *shape: pltpu.VMEM(shape, jnp.bfloat16)
    flops = 2 * tokens * (3 * hidden + 2 * features) * RANK
    return pl.pallas_call(
        project_kernel,
        out_shape=[half] * 4 + [jax.ShapeDtypeStruct((RANK, WIDE), jnp.bfloat16)],
        in_specs=[pl.BlockSpec(memory_space=pltpu.HBM)] * 11,
        out_specs=[inside] * 5,
        scratch_shapes=[
            buf(3, tokens, hidden),
            buf(2, tokens, features),
            buf(3, RANK, hidden),
            buf(2, RANK, features),
            buf(*query_grads.shape),
            pltpu.VMEM((3, tokens, WIDE), jnp.float32),
            pltpu.SemaphoreType.DMA((3, tokens // STRIP)),
            pltpu.SemaphoreType.DMA((8,)),
        ],
        compiler_params=pltpu.CompilerParams(vmem_limit_bytes=VMEM_BYTES),
        cost_estimate=pl.CostEstimate(flops=flops, bytes_accessed=17_000_000, transcendentals=tokens * hidden),
        name="project",
    )(gate_pre, up_pre, hidden_grad, layer_inputs, output_grad, *[pltpu.with_memory_space_constraint(v, pltpu.HBM) for v in (proj_in.T, proj_out.T, proj_gate.T, proj_up.T, proj_hidden.T, query_grads)])


def put_sum(out_ref, value):
    for i in range(TERMS):
        term = value.astype(jnp.bfloat16)
        out_ref[i * RANK : (i + 1) * RANK, :] = term
        value = value - term.astype(jnp.float32)


def get_sum(ref):
    terms = [ref[i * RANK : (i + 1) * RANK, :].astype(jnp.float32) for i in range(TERMS)]
    return (terms[2] + terms[1]) + terms[0]


def total_of(refs):
    parts = [get_sum(ref) for ref in refs]
    while len(parts) > 1:
        parts = [a + b for a, b in zip(parts[::2], parts[1::2])]
    return parts[0]


def gram_kernel(own_ref, a_ref, b_ref, c_ref, pieces_ref, message_ref, cross_ref):
    f32 = jnp.float32
    v = (own_ref[...].astype(f32) + a_ref[...].astype(f32)) + (b_ref[...].astype(f32) + c_ref[...].astype(f32))
    m = lax.dot_general(v, v, (((0,), (0,)), ((), ())), precision=HIGH, preferred_element_type=f32)
    left = lax.broadcasted_iota(jnp.int32, (RANK, WIDE), 1) < RANK
    put_sum(message_ref, jnp.where(left, m[:RANK], m[RANK:]))
    message_ref[FACTOR_ROWS:, :] = pieces_ref[...]
    cross_ref[...] = jnp.where(left, m[RANK:], m[:RANK])


def gram(parts, pieces):
    inside = pl.BlockSpec(memory_space=pltpu.VMEM)
    return pl.pallas_call(
        gram_kernel,
        out_shape=[
            jax.ShapeDtypeStruct((FACTOR_ROWS + pieces.shape[0], WIDE), jnp.bfloat16),
            jax.ShapeDtypeStruct((RANK, WIDE), jnp.float32),
        ],
        in_specs=[inside] * 5,
        out_specs=[inside] * 2,
        compiler_params=pltpu.CompilerParams(vmem_limit_bytes=SMALL_VMEM),
        name="gram",
    )(*parts, pieces)


def merge_kernel(*refs):
    parts, out_ref = refs[:-1], refs[-1]
    put_sum(out_ref, total_of(parts))
    rows = parts[0].shape[0] - FACTOR_ROWS
    for i, ref in enumerate(parts):
        out_ref[FACTOR_ROWS + i * rows : FACTOR_ROWS + (i + 1) * rows, :] = ref[FACTOR_ROWS:, :]


def merge(parts):
    inside = pl.BlockSpec(memory_space=pltpu.VMEM)
    rows = FACTOR_ROWS + len(parts) * (parts[0].shape[0] - FACTOR_ROWS)
    return pl.pallas_call(
        merge_kernel,
        out_shape=jax.ShapeDtypeStruct((rows, WIDE), jnp.bfloat16),
        in_specs=[inside] * len(parts),
        out_specs=inside,
        compiler_params=pltpu.CompilerParams(vmem_limit_bytes=SMALL_VMEM),
        name="merge",
    )(*parts)


def solve_two(m, rows):
    (a, b), (c, d) = m
    scale = 1.0 / (a * d - b * c)
    a, b, c, d = d * scale, b * scale, c * scale, a * scale
    return a * rows[0] - b * rows[1], d * rows[1] - c * rows[0]


def invert_pair(w):
    lane = lax.broadcasted_iota(jnp.int32, (RANK, WIDE), 1)
    row_at = lax.broadcasted_iota(jnp.int32, (RANK, WIDE), 0)
    left = lane < RANK
    column_at = jnp.where(left, lane, lane - RANK)

    def column(k):
        return jnp.where(
            left,
            jnp.broadcast_to(w[:, k : k + 1], (RANK, WIDE)),
            jnp.broadcast_to(w[:, RANK + k : RANK + k + 1], (RANK, WIDE)),
        )

    for k in range(0, RANK, 4):
        cols = [column(k + i) for i in range(4)]
        m = [[c[k + i : k + i + 1] for c in cols] for i in range(4)]
        at = column_at[:1]
        rows = [
            jnp.where((at >= k) & (at < k + 4), jnp.where(at == k + i, 1.0, 0.0), w[k + i : k + i + 1])
            for i in range(4)
        ]
        upper = [m[0][:2], m[1][:2]]
        x0, x1 = solve_two(upper, rows[:2])
        e02, e12 = solve_two(upper, (m[0][2], m[1][2]))
        e03, e13 = solve_two(upper, (m[0][3], m[1][3]))
        rest = [[m[i][2] - m[i][0] * e02 - m[i][1] * e12, m[i][3] - m[i][0] * e03 - m[i][1] * e13] for i in (2, 3)]
        n2, n3 = solve_two(rest, [rows[i] - m[i][0] * x0 - m[i][1] * x1 for i in (2, 3)])
        new = [x0 - e02 * n2 - e03 * n3, x1 - e12 * n2 - e13 * n3, n2, n3]
        out = jnp.where((column_at >= k) & (column_at < k + 4), 0.0, w)
        out = (out - cols[0] * new[0] - cols[1] * new[1]) - (cols[2] * new[2] + cols[3] * new[3])
        for i in range(4):
            out = jnp.where(row_at == k + i, new[i], out)
        w = out
    return w


def score_kernel(count, cross_ref, *refs):
    parts, out_ref = refs[:-1], refs[-1]
    f32 = jnp.float32
    lane = lax.broadcasted_iota(jnp.int32, (RANK, WIDE), 1)
    row_at = lax.broadcasted_iota(jnp.int32, (RANK, WIDE), 0)
    diag = (lane == row_at) | (lane == row_at + RANK)
    inv = invert_pair(total_of(parts) * (1.0 / count) + jnp.where(diag, DAMP, 0.0))
    dot = lambda a, b: jnp.dot(a, b, precision=HIGH, preferred_element_type=f32)
    h = dot(dot(inv[:, :RANK], cross_ref[:, RANK:]), inv[:, RANK:])
    h = jnp.concatenate([h[: RANK // 2], h[RANK // 2 :]], axis=1).reshape(1, SIDE, 8, WIDE)
    sums = []
    for ref in parts:
        q = ref[FACTOR_ROWS:, :].astype(f32)
        q = q.reshape(q.shape[0] // (RANK // 2), SIDE, 8, WIDE)
        sums.append((q * h).sum(axis=1).reshape(q.shape[0] * 8, WIDE))
    sums = jnp.concatenate(sums, axis=0)
    queries = sums.shape[0] // 8
    me = lax.axis_index("dp")
    j = lax.shift_right_logical(lax.broadcasted_iota(jnp.int32, (queries, sums.shape[0]), 1), 3)
    want = lax.broadcasted_iota(jnp.int32, (queries, sums.shape[0]), 0)
    last, middle = lax.shift_right_logical(j, 5), lax.shift_right_logical(j, 3)
    swap = (lax.axis_index("tensor") & 1) == 1
    y = (lax.shift_right_logical(me, 4) - jnp.where(swap, middle, last)) & 3
    x = (lax.shift_right_logical(me, 2) - jnp.where(swap, last, middle)) & 3
    step = lax.shift_right_logical(j, 1) & 3
    z = (me & 3) ^ step ^ lax.shift_right_logical(step, 1)
    source = y * 32 + x * 8 + z * 2 + (j & 1)
    place = jnp.where(source == want, 1.0, 0.0).astype(f32)
    by_query = dot(place, sums)
    ones = jnp.full((8, WIDE), 1.0 / (RANK * RANK), f32)
    row = lax.dot_general(ones, by_query, (((1,), (1,)), ((), ())), precision=HIGH, preferred_element_type=f32)
    out_ref[...] = jnp.where(lax.axis_index("tensor") == 3, 0.0, row[:1])


def score(count, cross, parts):
    inside = pl.BlockSpec(memory_space=pltpu.VMEM)
    total = sum(p.shape[0] - FACTOR_ROWS for p in parts) // (RANK // 2)
    return pl.pallas_call(
        lambda *refs: score_kernel(count, *refs),
        out_shape=jax.ShapeDtypeStruct((1, total), jnp.float32),
        in_specs=[inside] * (1 + SIDE),
        out_specs=inside,
        compiler_params=pltpu.CompilerParams(vmem_limit_bytes=SMALL_VMEM),
        name="score",
    )(cross, *parts)


def ring(names, step, size):
    def to(i, t):
        stride = RINGS[names[t & 1]]
        at = (i // stride) % SIDE
        return (i + ((at + step) % SIDE - at) * stride) * 4 + t

    return [(i * 4 + t, to(i, t)) for i in range(size) for t in range(4)]


def flipped(stride, mask, size):
    def to(i):
        at = (i // stride) % SIDE
        return i + ((at ^ mask) - at) * stride

    return [(i, to(i)) for i in range(size)]


def body(
    layer_inputs, gate_pre, up_pre, hidden_grad, output_grad,
    proj_in, proj_out, proj_gate, proj_up, proj_hidden, query_grads,
):
    size = lax.axis_size("dp")

    def around(value, names):
        far, near, back = [lax.ppermute(value, ("dp", "tensor"), ring(names, s, size)) for s in (2, 1, 3)]
        return [value, near, far, back]

    def shifted(value, step):
        return lax.ppermute(value, "tensor", [(i, (i + step) % 4) for i in range(4)])

    stay = lambda v: pltpu.with_memory_space_constraint(v, pltpu.HBM)
    gate_pre, up_pre, hidden_grad, layer_inputs, output_grad = map(stay, (gate_pre, up_pre, hidden_grad, layer_inputs, output_grad))
    own, nxt, across, last, pieces = project(
        gate_pre, up_pre, hidden_grad, layer_inputs, output_grad,
        proj_in, proj_out, proj_gate, proj_up, proj_hidden, query_grads,
    )
    message, cross = gram((own, shifted(nxt, 1), shifted(across, 2), shifted(last, 3)), pieces)
    for mask in (1, 3):
        message = merge([message, lax.ppermute(message, "dp", flipped(RINGS["z"], mask, size))])
    message = merge(around(message, "xy"))
    part = score(layer_inputs.shape[0] * size, cross, around(message, "yx"))
    parts = [part] + [shifted(part, s) for s in (1, 2, 3)]
    at = lax.axis_index("tensor")

    def of(index):
        picked = parts[3]
        for s in (2, 1, 0):
            picked = jnp.where((at - index) % 4 == s, parts[s], picked)
        return picked

    return ((of(0) + of(1)) + of(2)).reshape(-1, 1)


def solution(mesh):
    placed = (
        P("dp", "tensor"), P("dp", "tensor"), P("dp", "tensor"), P("dp", "tensor"), P("dp", "tensor"),
        P(), P(), P("tensor", None), P("tensor", None), P("tensor", None),
        P("dp", None, None, None),
    )
    return jax.shard_map(body, mesh=mesh, in_specs=placed, out_specs=P(None, "dp"), check_vma=False)
```

```python
import jax
import jax.numpy as jnp
from jax import lax
from jax.experimental import pallas as pl
from jax.experimental.pallas import tpu as pltpu
from jax.sharding import PartitionSpec as P

HIGH = lax.Precision.HIGHEST
DAMP = 0.1
RANK = 64
WIDE = 2 * RANK
STRIP = 128
AHEAD = 3
SIDE = 4
VMEM_BYTES = 32 * 1024 * 1024

TERMS = 3
FACTOR_ROWS = TERMS * RANK
SMALL_VMEM = 32 * 1024 * 1024
RINGS = {"y": 16, "x": 4, "z": 1}


def layer_of(tensor_at):
    return lax.rem(tensor_at, 3)


def rows_dot(a, b):
    return lax.dot_general(a, b, (((1,), (1,)), ((), ())), preferred_element_type=jnp.float32)


def project_kernel(
    gate_hbm, up_hbm, grad_hbm, inputs_hbm, outg_hbm,
    win_hbm, wout_hbm, wgate_hbm, wup_hbm, whid_hbm, query_hbm,
    own_ref, next_ref, across_ref, last_ref, pieces_ref,
    hidden_buf, side_buf, hidden_w, side_w, query_buf, sums, sems, side_sems,
):
    tensor_at = lax.axis_index("tensor")
    tokens, hidden = gate_hbm.shape
    features = inputs_hbm.shape[1]
    strips = tokens // STRIP

    def side_copies():
        mine = pl.ds(pl.multiple_of(tensor_at * features, features), features)
        return [
            pltpu.make_async_copy(src, side_buf.at[i], side_sems.at[i])
            for i, src in enumerate((inputs_hbm, outg_hbm))
        ] + [
            pltpu.make_async_copy(src.at[:, mine], side_w.at[i], side_sems.at[2 + i])
            for i, src in enumerate((win_hbm, wout_hbm))
        ]

    def weight_copies():
        return [
            pltpu.make_async_copy(src, hidden_w.at[i], side_sems.at[5 + i])
            for i, src in enumerate((wgate_hbm, wup_hbm, whid_hbm))
        ]

    def chunk_copies(c):
        rows = pl.ds(pl.multiple_of(c * STRIP, STRIP), STRIP)
        return [
            pltpu.make_async_copy(src.at[rows, :], hidden_buf.at[i, rows, :], sems.at[i, c])
            for i, src in enumerate((gate_hbm, up_hbm, grad_hbm))
        ]

    def start(copies):
        for copy in copies:
            copy.start()

    def arrive(copies):
        for copy in copies:
            copy.wait()

    query_copy = pltpu.make_async_copy(query_hbm, query_buf, side_sems.at[4])
    query_copy.start()
    start(weight_copies())
    start(chunk_copies(0))

    @pl.loop(0, strips)
    def _(c):
        arrive(chunk_copies(c))

        @pl.when(c == 0)
        def _():
            for k in range(1, 3):
                start(chunk_copies(k))
            arrive(weight_copies())

        @pl.when((c > 0) & (c + 2 < strips))
        def _():
            start(chunk_copies(c + 2))

        @pl.when(c == 2)
        def _():
            start(side_copies())

        at = pl.ds(pl.multiple_of(c * STRIP, STRIP), STRIP)
        g = hidden_buf[0, at, :].astype(jnp.float32)
        u = hidden_buf[1, at, :].astype(jnp.float32)
        e = hidden_buf[2, at, :].astype(jnp.float32)
        th = jnp.tanh(0.5 * g)
        p, q = 1.0 + th, 1.0 - th
        a = g * p
        gate_grad = ((e * u) * (p * (2.0 + g * q))).astype(jnp.bfloat16)
        up_grad = (e * a).astype(jnp.bfloat16)
        hid = (a * u).astype(jnp.bfloat16)
        for i, act in enumerate((gate_grad, up_grad, hid)):
            sums[i, at, :RANK] = rows_dot(act, hidden_w[i]) * (0.25 if i == 0 else 0.5)

    arrive(side_copies())

    @pl.loop(0, 2)
    def _(i):
        sums[2 * i, :, RANK:] = rows_dot(side_buf[i], side_w[i])

    query_copy.wait()
    layer = layer_of(tensor_at)
    for q in range(2):
        rows = query_buf[q, layer].astype(jnp.float32)
        rows = jnp.where(layer == 2, rows.T, rows)
        packed = jnp.concatenate([rows[: RANK // 2], rows[RANK // 2 :]], axis=1)
        pieces_ref[q * (RANK // 2) : (q + 1) * (RANK // 2), :] = packed.astype(jnp.bfloat16)

    sums[1, :, RANK:] = sums[0, :, RANK:]
    for s, out in enumerate((own_ref, next_ref, across_ref, last_ref)):
        out[...] = sums[layer_of(lax.rem(tensor_at + s, 4))].astype(jnp.bfloat16)


def project(gate_pre, up_pre, hidden_grad, layer_inputs, output_grad, proj_in, proj_out, proj_gate, proj_up, proj_hidden, query_grads):
    tokens, hidden = gate_pre.shape
    features = layer_inputs.shape[1]
    half = jax.ShapeDtypeStruct((tokens, WIDE), jnp.bfloat16)
    inside = pl.BlockSpec(memory_space=pltpu.VMEM)
    buf = lambda *shape: pltpu.VMEM(shape, jnp.bfloat16)
    flops = 2 * tokens * (3 * hidden + 2 * features) * RANK
    return pl.pallas_call(
        project_kernel,
        out_shape=[half] * 4 + [jax.ShapeDtypeStruct((RANK, WIDE), jnp.bfloat16)],
        in_specs=[pl.BlockSpec(memory_space=pltpu.HBM)] * 11,
        out_specs=[inside] * 5,
        scratch_shapes=[
            buf(3, tokens, hidden),
            buf(2, tokens, features),
            buf(3, RANK, hidden),
            buf(2, RANK, features),
            buf(*query_grads.shape),
            pltpu.VMEM((3, tokens, WIDE), jnp.float32),
            pltpu.SemaphoreType.DMA((3, tokens // STRIP)),
            pltpu.SemaphoreType.DMA((8,)),
        ],
        compiler_params=pltpu.CompilerParams(vmem_limit_bytes=VMEM_BYTES),
        cost_estimate=pl.CostEstimate(flops=flops, bytes_accessed=17_000_000, transcendentals=tokens * hidden),
        name="project",
    )(gate_pre, up_pre, hidden_grad, layer_inputs, output_grad, *[pltpu.with_memory_space_constraint(v, pltpu.HBM) for v in (proj_in.T, proj_out.T, proj_gate.T, proj_up.T, proj_hidden.T, query_grads)])


def put_sum(out_ref, value):
    for i in range(TERMS):
        term = value.astype(jnp.bfloat16)
        out_ref[i * RANK : (i + 1) * RANK, :] = term
        value = value - term.astype(jnp.float32)


def get_sum(ref):
    terms = [ref[i * RANK : (i + 1) * RANK, :].astype(jnp.float32) for i in range(TERMS)]
    return (terms[2] + terms[1]) + terms[0]


def total_of(refs):
    parts = [get_sum(ref) for ref in refs]
    while len(parts) > 1:
        parts = [a + b for a, b in zip(parts[::2], parts[1::2])]
    return parts[0]


def gram_kernel(own_ref, a_ref, b_ref, c_ref, pieces_ref, message_ref, cross_ref):
    f32 = jnp.float32
    v = (own_ref[...].astype(f32) + a_ref[...].astype(f32)) + (b_ref[...].astype(f32) + c_ref[...].astype(f32))
    m = lax.dot_general(v, v, (((0,), (0,)), ((), ())), precision=HIGH, preferred_element_type=f32)
    left = lax.broadcasted_iota(jnp.int32, (RANK, WIDE), 1) < RANK
    put_sum(message_ref, jnp.where(left, m[:RANK], m[RANK:]))
    message_ref[FACTOR_ROWS:, :] = pieces_ref[...]
    cross_ref[...] = jnp.where(left, m[RANK:], m[:RANK])


def gram(parts, pieces):
    inside = pl.BlockSpec(memory_space=pltpu.VMEM)
    return pl.pallas_call(
        gram_kernel,
        out_shape=[
            jax.ShapeDtypeStruct((FACTOR_ROWS + pieces.shape[0], WIDE), jnp.bfloat16),
            jax.ShapeDtypeStruct((RANK, WIDE), jnp.float32),
        ],
        in_specs=[inside] * 5,
        out_specs=[inside] * 2,
        compiler_params=pltpu.CompilerParams(vmem_limit_bytes=SMALL_VMEM),
        name="gram",
    )(*parts, pieces)


def merge_kernel(*refs):
    parts, out_ref = refs[:-1], refs[-1]
    put_sum(out_ref, total_of(parts))
    rows = parts[0].shape[0] - FACTOR_ROWS
    for i, ref in enumerate(parts):
        out_ref[FACTOR_ROWS + i * rows : FACTOR_ROWS + (i + 1) * rows, :] = ref[FACTOR_ROWS:, :]


def merge(parts):
    inside = pl.BlockSpec(memory_space=pltpu.VMEM)
    rows = FACTOR_ROWS + len(parts) * (parts[0].shape[0] - FACTOR_ROWS)
    return pl.pallas_call(
        merge_kernel,
        out_shape=jax.ShapeDtypeStruct((rows, WIDE), jnp.bfloat16),
        in_specs=[inside] * len(parts),
        out_specs=inside,
        compiler_params=pltpu.CompilerParams(vmem_limit_bytes=SMALL_VMEM),
        name="merge",
    )(*parts)


def solve_two(m, rows):
    (a, b), (c, d) = m
    scale = 1.0 / (a * d - b * c)
    a, b, c, d = d * scale, b * scale, c * scale, a * scale
    return a * rows[0] - b * rows[1], d * rows[1] - c * rows[0]


def invert_pair(w):
    lane = lax.broadcasted_iota(jnp.int32, (RANK, WIDE), 1)
    row_at = lax.broadcasted_iota(jnp.int32, (RANK, WIDE), 0)
    left = lane < RANK
    column_at = jnp.where(left, lane, lane - RANK)

    def column(k):
        return jnp.where(
            left,
            jnp.broadcast_to(w[:, k : k + 1], (RANK, WIDE)),
            jnp.broadcast_to(w[:, RANK + k : RANK + k + 1], (RANK, WIDE)),
        )

    for k in range(0, RANK, 4):
        cols = [column(k + i) for i in range(4)]
        m = [[c[k + i : k + i + 1] for c in cols] for i in range(4)]
        at = column_at[:1]
        rows = [
            jnp.where((at >= k) & (at < k + 4), jnp.where(at == k + i, 1.0, 0.0), w[k + i : k + i + 1])
            for i in range(4)
        ]
        upper = [m[0][:2], m[1][:2]]
        x0, x1 = solve_two(upper, rows[:2])
        e02, e12 = solve_two(upper, (m[0][2], m[1][2]))
        e03, e13 = solve_two(upper, (m[0][3], m[1][3]))
        rest = [[m[i][2] - m[i][0] * e02 - m[i][1] * e12, m[i][3] - m[i][0] * e03 - m[i][1] * e13] for i in (2, 3)]
        n2, n3 = solve_two(rest, [rows[i] - m[i][0] * x0 - m[i][1] * x1 for i in (2, 3)])
        new = [x0 - e02 * n2 - e03 * n3, x1 - e12 * n2 - e13 * n3, n2, n3]
        out = jnp.where((column_at >= k) & (column_at < k + 4), 0.0, w)
        out = (out - cols[0] * new[0] - cols[1] * new[1]) - (cols[2] * new[2] + cols[3] * new[3])
        for i in range(4):
            out = jnp.where(row_at == k + i, new[i], out)
        w = out
    return w


def score_kernel(count, cross_ref, *refs):
    parts, out_ref = refs[:-1], refs[-1]
    f32 = jnp.float32
    lane = lax.broadcasted_iota(jnp.int32, (RANK, WIDE), 1)
    row_at = lax.broadcasted_iota(jnp.int32, (RANK, WIDE), 0)
    diag = (lane == row_at) | (lane == row_at + RANK)
    inv = invert_pair(total_of(parts) * (1.0 / count) + jnp.where(diag, DAMP, 0.0))
    dot = lambda a, b: jnp.dot(a, b, precision=HIGH, preferred_element_type=f32)
    h = dot(dot(inv[:, :RANK], cross_ref[:, RANK:]), inv[:, RANK:])
    h = jnp.concatenate([h[: RANK // 2], h[RANK // 2 :]], axis=1).reshape(1, SIDE, 8, WIDE)
    sums = []
    for ref in parts:
        q = ref[FACTOR_ROWS:, :].astype(f32)
        q = q.reshape(q.shape[0] // (RANK // 2), SIDE, 8, WIDE)
        sums.append((q * h).sum(axis=1).sum(axis=1))
    sums = jnp.concatenate(sums, axis=0)
    queries = sums.shape[0]
    me = lax.axis_index("dp")
    j = lax.broadcasted_iota(jnp.int32, (queries, queries), 0)
    want = lax.broadcasted_iota(jnp.int32, (queries, queries), 1)
    last, middle = lax.shift_right_logical(j, 5), lax.shift_right_logical(j, 3)
    swap = (lax.axis_index("tensor") & 1) == 1
    y = (lax.shift_right_logical(me, 4) - jnp.where(swap, middle, last)) & 3
    x = (lax.shift_right_logical(me, 2) - jnp.where(swap, last, middle)) & 3
    step = lax.shift_right_logical(j, 1) & 3
    z = (me & 3) ^ step ^ lax.shift_right_logical(step, 1)
    source = y * 32 + x * 8 + z * 2 + (j & 1)
    place = jnp.where(source == want, 1.0, 0.0).astype(f32)
    by_row = sums.sum(axis=1, keepdims=True) * (1.0 / (RANK * RANK))
    row = (place * by_row).sum(axis=0, keepdims=True)
    out_ref[...] = jnp.where(lax.axis_index("tensor") == 3, 0.0, row)


def score(count, cross, parts):
    inside = pl.BlockSpec(memory_space=pltpu.VMEM)
    total = sum(p.shape[0] - FACTOR_ROWS for p in parts) // (RANK // 2)
    return pl.pallas_call(
        lambda *refs: score_kernel(count, *refs),
        out_shape=jax.ShapeDtypeStruct((1, total), jnp.float32),
        in_specs=[inside] * (1 + SIDE),
        out_specs=inside,
        compiler_params=pltpu.CompilerParams(vmem_limit_bytes=SMALL_VMEM),
        name="score",
    )(cross, *parts)


def ring(names, step, size):
    def to(i, t):
        stride = RINGS[names[t & 1]]
        at = (i // stride) % SIDE
        return (i + ((at + step) % SIDE - at) * stride) * 4 + t

    return [(i * 4 + t, to(i, t)) for i in range(size) for t in range(4)]


def flipped(stride, mask, size):
    def to(i):
        at = (i // stride) % SIDE
        return i + ((at ^ mask) - at) * stride

    return [(i, to(i)) for i in range(size)]


def body(
    layer_inputs, gate_pre, up_pre, hidden_grad, output_grad,
    proj_in, proj_out, proj_gate, proj_up, proj_hidden, query_grads,
):
    size = lax.axis_size("dp")

    def around(value, names):
        far, near, back = [lax.ppermute(value, ("dp", "tensor"), ring(names, s, size)) for s in (2, 1, 3)]
        return [value, near, far, back]

    def shifted(value, step):
        return lax.ppermute(value, "tensor", [(i, (i + step) % 4) for i in range(4)])

    stay = lambda v: pltpu.with_memory_space_constraint(v, pltpu.HBM)
    gate_pre, up_pre, hidden_grad, layer_inputs, output_grad = map(stay, (gate_pre, up_pre, hidden_grad, layer_inputs, output_grad))
    own, nxt, across, last, pieces = project(
        gate_pre, up_pre, hidden_grad, layer_inputs, output_grad,
        proj_in, proj_out, proj_gate, proj_up, proj_hidden, query_grads,
    )
    message, cross = gram((own, shifted(nxt, 1), shifted(across, 2), shifted(last, 3)), pieces)
    for mask in (1, 3):
        message = merge([message, lax.ppermute(message, "dp", flipped(RINGS["z"], mask, size))])
    message = merge(around(message, "xy"))
    part = score(layer_inputs.shape[0] * size, cross, around(message, "yx"))
    parts = [part] + [shifted(part, s) for s in (1, 2, 3)]
    at = lax.axis_index("tensor")

    def of(index):
        picked = parts[3]
        for s in (2, 1, 0):
            picked = jnp.where((at - index) % 4 == s, parts[s], picked)
        return picked

    return ((of(0) + of(1)) + of(2)).reshape(-1, 1)


def solution(mesh):
    placed = (
        P("dp", "tensor"), P("dp", "tensor"), P("dp", "tensor"), P("dp", "tensor"), P("dp", "tensor"),
        P(), P(), P("tensor", None), P("tensor", None), P("tensor", None),
        P("dp", None, None, None),
    )
    return jax.shard_map(body, mesh=mesh, in_specs=placed, out_specs=P(None, "dp"), check_vma=False)
```

```python
import jax
import jax.numpy as jnp
from jax import lax
from jax.experimental import pallas as pl
from jax.experimental.pallas import tpu as pltpu
from jax.sharding import PartitionSpec as P

HIGH = lax.Precision.HIGHEST
DAMP = 0.1
RANK = 64
WIDE = 2 * RANK
STRIP = 128
AHEAD = 3
SIDE = 4
VMEM_BYTES = 32 * 1024 * 1024

TERMS = 3
FACTOR_ROWS = TERMS * RANK
SMALL_VMEM = 32 * 1024 * 1024
RINGS = {"y": 16, "x": 4, "z": 1}


def layer_of(tensor_at):
    return jnp.minimum(tensor_at, 2)


def rows_dot(a, b):
    return lax.dot_general(a, b, (((1,), (1,)), ((), ())), preferred_element_type=jnp.float32)


def project_kernel(
    gate_hbm, up_hbm, grad_hbm, inputs_hbm, outg_hbm,
    win_hbm, wout_hbm, wgate_hbm, wup_hbm, whid_hbm, query_hbm,
    own_ref, core_ref, pieces_ref,
    hidden_buf, side_buf, hidden_w, side_w, query_buf, sums, sems, side_sems,
):
    tensor_at = lax.axis_index("tensor")
    tokens, hidden = gate_hbm.shape
    features = inputs_hbm.shape[1]
    strips = tokens // STRIP

    def weight_copies():
        mine = pl.ds(pl.multiple_of(tensor_at * features, features), features)
        return [
            pltpu.make_async_copy(src.at[:, mine], side_w.at[i], side_sems.at[2 + i])
            for i, src in enumerate((win_hbm, wout_hbm))
        ] + [
            pltpu.make_async_copy(src, hidden_w.at[i], side_sems.at[5 + i])
            for i, src in enumerate((wgate_hbm, wup_hbm, whid_hbm))
        ]

    def chunk_copies(c):
        rows = pl.ds(pl.multiple_of(c * STRIP, STRIP), STRIP)
        return [
            pltpu.make_async_copy(src.at[rows, :], hidden_buf.at[i, rows, :], sems.at[i, c])
            for i, src in enumerate((gate_hbm, up_hbm, grad_hbm))
        ] + [
            pltpu.make_async_copy(src.at[rows, :], side_buf.at[i, rows, :], sems.at[3 + i, c])
            for i, src in enumerate((inputs_hbm, outg_hbm))
        ]

    def start(copies):
        for copy in copies:
            copy.start()

    def arrive(copies):
        for copy in copies:
            copy.wait()

    query_copy = pltpu.make_async_copy(query_hbm, query_buf, side_sems.at[4])
    query_copy.start()
    start(weight_copies())
    start(chunk_copies(0))

    @pl.loop(0, strips)
    def _(c):
        arrive(chunk_copies(c))

        @pl.when(c == 0)
        def _():
            for k in range(1, 3):
                start(chunk_copies(k))
            arrive(weight_copies())

        @pl.when((c > 0) & (c + 2 < strips))
        def _():
            start(chunk_copies(c + 2))

        at = pl.ds(pl.multiple_of(c * STRIP, STRIP), STRIP)
        g = hidden_buf[0, at, :].astype(jnp.float32)
        u = hidden_buf[1, at, :].astype(jnp.float32)
        e = hidden_buf[2, at, :].astype(jnp.float32)
        th = jnp.tanh(0.5 * g)
        p, q = 1.0 + th, 1.0 - th
        a = g * p
        gate_grad = ((e * u) * (p * (2.0 + g * q))).astype(jnp.bfloat16)
        up_grad = (e * a).astype(jnp.bfloat16)
        hid = (a * u).astype(jnp.bfloat16)
        for i, act in enumerate((gate_grad, up_grad, hid)):
            sums[i, at, :RANK] = rows_dot(act, hidden_w[i]) * (0.25 if i == 0 else 0.5)
        for i in range(2):
            sums[2 * i, at, RANK:] = rows_dot(side_buf[i, at, :], side_w[i])

    query_copy.wait()
    layer = layer_of(tensor_at)
    for q in range(2):
        rows = query_buf[q, layer].astype(jnp.float32)
        rows = jnp.where(layer == 2, rows.T, rows)
        packed = jnp.concatenate([rows[: RANK // 2], rows[RANK // 2 :]], axis=1)
        pieces_ref[q * (RANK // 2) : (q + 1) * (RANK // 2), :] = packed.astype(jnp.bfloat16)

    sums[1, :, RANK:] = sums[0, :, RANK:]
    core = tensor_at & 1
    core_ref[:tokens, :] = sums[1 - core].astype(jnp.bfloat16)
    core_ref[tokens:, :] = sums[2].astype(jnp.bfloat16)
    own_ref[:tokens, :] = sums[core]
    own_ref[tokens:, :] = sums[2]


def project(gate_pre, up_pre, hidden_grad, layer_inputs, output_grad, proj_in, proj_out, proj_gate, proj_up, proj_hidden, query_grads):
    tokens, hidden = gate_pre.shape
    features = layer_inputs.shape[1]
    inside = pl.BlockSpec(memory_space=pltpu.VMEM)
    buf = lambda *shape: pltpu.VMEM(shape, jnp.bfloat16)
    flops = 2 * tokens * (3 * hidden + 2 * features) * RANK
    return pl.pallas_call(
        project_kernel,
        out_shape=[
            jax.ShapeDtypeStruct((2 * tokens, WIDE), jnp.float32),
            jax.ShapeDtypeStruct((2 * tokens, WIDE), jnp.bfloat16),
            jax.ShapeDtypeStruct((RANK, WIDE), jnp.bfloat16),
        ],
        in_specs=[pl.BlockSpec(memory_space=pltpu.HBM)] * 11,
        out_specs=[inside] * 3,
        scratch_shapes=[
            buf(3, tokens, hidden),
            buf(2, tokens, features),
            buf(3, RANK, hidden),
            buf(2, RANK, features),
            buf(*query_grads.shape),
            pltpu.VMEM((3, tokens, WIDE), jnp.float32),
            pltpu.SemaphoreType.DMA((5, tokens // STRIP)),
            pltpu.SemaphoreType.DMA((8,)),
        ],
        compiler_params=pltpu.CompilerParams(vmem_limit_bytes=VMEM_BYTES),
        cost_estimate=pl.CostEstimate(flops=flops, bytes_accessed=17_000_000, transcendentals=tokens * hidden),
        name="project",
    )(gate_pre, up_pre, hidden_grad, layer_inputs, output_grad, *[pltpu.with_memory_space_constraint(v, pltpu.HBM) for v in (proj_in.T, proj_out.T, proj_gate.T, proj_up.T, proj_hidden.T, query_grads)])


def put_sum(out_ref, value):
    for i in range(TERMS):
        term = value.astype(jnp.bfloat16)
        out_ref[i * RANK : (i + 1) * RANK, :] = term
        value = value - term.astype(jnp.float32)


def get_sum(ref):
    terms = [ref[i * RANK : (i + 1) * RANK, :].astype(jnp.float32) for i in range(TERMS)]
    return (terms[2] + terms[1]) + terms[0]


def total_of(refs):
    parts = [get_sum(ref) for ref in refs]
    while len(parts) > 1:
        parts = [a + b for a, b in zip(parts[::2], parts[1::2])]
    return parts[0]


def chip_kernel(own_ref, core_ref, keep_ref, send_ref):
    tokens = keep_ref.shape[0]
    far = lax.shift_right_logical(lax.axis_index("tensor"), 1)
    kept, sent = [pl.ds(pl.multiple_of(at * tokens, tokens), tokens) for at in (far, 1 - far)]
    keep_ref[...] = own_ref[kept, :] + core_ref[kept, :].astype(jnp.float32)
    send_ref[...] = (own_ref[sent, :] + core_ref[sent, :].astype(jnp.float32)).astype(jnp.bfloat16)


def chip_sums(own, core):
    inside = pl.BlockSpec(memory_space=pltpu.VMEM)
    shape = (own.shape[0] // 2, own.shape[1])
    return pl.pallas_call(
        chip_kernel,
        out_shape=[jax.ShapeDtypeStruct(shape, jnp.float32), jax.ShapeDtypeStruct(shape, jnp.bfloat16)],
        in_specs=[inside] * 2,
        out_specs=[inside] * 2,
        compiler_params=pltpu.CompilerParams(vmem_limit_bytes=SMALL_VMEM),
        name="chip_sums",
    )(own, core)


def gram_kernel(keep_ref, got_ref, pieces_ref, message_ref, cross_ref):
    f32 = jnp.float32
    v = keep_ref[...] + got_ref[...].astype(f32)
    m = lax.dot_general(v, v, (((0,), (0,)), ((), ())), precision=HIGH, preferred_element_type=f32)
    left = lax.broadcasted_iota(jnp.int32, (RANK, WIDE), 1) < RANK
    put_sum(message_ref, jnp.where(left, m[:RANK], m[RANK:]))
    message_ref[FACTOR_ROWS:, :] = pieces_ref[...]
    cross_ref[...] = jnp.where(left, m[RANK:], m[:RANK])


def gram(parts, pieces):
    inside = pl.BlockSpec(memory_space=pltpu.VMEM)
    return pl.pallas_call(
        gram_kernel,
        out_shape=[
            jax.ShapeDtypeStruct((FACTOR_ROWS + pieces.shape[0], WIDE), jnp.bfloat16),
            jax.ShapeDtypeStruct((RANK, WIDE), jnp.float32),
        ],
        in_specs=[inside] * 3,
        out_specs=[inside] * 2,
        compiler_params=pltpu.CompilerParams(vmem_limit_bytes=SMALL_VMEM),
        name="gram",
    )(*parts, pieces)


def merge_kernel(*refs):
    parts, out_ref = refs[:-1], refs[-1]
    put_sum(out_ref, total_of(parts))
    rows = parts[0].shape[0] - FACTOR_ROWS
    for i, ref in enumerate(parts):
        out_ref[FACTOR_ROWS + i * rows : FACTOR_ROWS + (i + 1) * rows, :] = ref[FACTOR_ROWS:, :]


def merge(parts):
    inside = pl.BlockSpec(memory_space=pltpu.VMEM)
    rows = FACTOR_ROWS + len(parts) * (parts[0].shape[0] - FACTOR_ROWS)
    return pl.pallas_call(
        merge_kernel,
        out_shape=jax.ShapeDtypeStruct((rows, WIDE), jnp.bfloat16),
        in_specs=[inside] * len(parts),
        out_specs=inside,
        compiler_params=pltpu.CompilerParams(vmem_limit_bytes=SMALL_VMEM),
        name="merge",
    )(*parts)


def solve_two(m, rows):
    (a, b), (c, d) = m
    scale = 1.0 / (a * d - b * c)
    a, b, c, d = d * scale, b * scale, c * scale, a * scale
    return a * rows[0] - b * rows[1], d * rows[1] - c * rows[0]


def invert_pair(w):
    lane = lax.broadcasted_iota(jnp.int32, (RANK, WIDE), 1)
    row_at = lax.broadcasted_iota(jnp.int32, (RANK, WIDE), 0)
    left = lane < RANK
    column_at = jnp.where(left, lane, lane - RANK)

    def column(k):
        return jnp.where(
            left,
            jnp.broadcast_to(w[:, k : k + 1], (RANK, WIDE)),
            jnp.broadcast_to(w[:, RANK + k : RANK + k + 1], (RANK, WIDE)),
        )

    for k in range(0, RANK, 4):
        cols = [column(k + i) for i in range(4)]
        m = [[c[k + i : k + i + 1] for c in cols] for i in range(4)]
        at = column_at[:1]
        rows = [
            jnp.where((at >= k) & (at < k + 4), jnp.where(at == k + i, 1.0, 0.0), w[k + i : k + i + 1])
            for i in range(4)
        ]
        upper = [m[0][:2], m[1][:2]]
        x0, x1 = solve_two(upper, rows[:2])
        e02, e12 = solve_two(upper, (m[0][2], m[1][2]))
        e03, e13 = solve_two(upper, (m[0][3], m[1][3]))
        rest = [[m[i][2] - m[i][0] * e02 - m[i][1] * e12, m[i][3] - m[i][0] * e03 - m[i][1] * e13] for i in (2, 3)]
        n2, n3 = solve_two(rest, [rows[i] - m[i][0] * x0 - m[i][1] * x1 for i in (2, 3)])
        new = [x0 - e02 * n2 - e03 * n3, x1 - e12 * n2 - e13 * n3, n2, n3]
        out = jnp.where((column_at >= k) & (column_at < k + 4), 0.0, w)
        out = (out - cols[0] * new[0] - cols[1] * new[1]) - (cols[2] * new[2] + cols[3] * new[3])
        for i in range(4):
            out = jnp.where(row_at == k + i, new[i], out)
        w = out
    return w


def score_kernel(count, cross_ref, *refs):
    parts, out_ref = refs[:-1], refs[-1]
    f32 = jnp.float32
    lane = lax.broadcasted_iota(jnp.int32, (RANK, WIDE), 1)
    row_at = lax.broadcasted_iota(jnp.int32, (RANK, WIDE), 0)
    diag = (lane == row_at) | (lane == row_at + RANK)
    inv = invert_pair(total_of(parts) * (1.0 / count) + jnp.where(diag, DAMP, 0.0))
    dot = lambda a, b: jnp.dot(a, b, precision=HIGH, preferred_element_type=f32)
    h = dot(dot(inv[:, :RANK], cross_ref[:, RANK:]), inv[:, RANK:])
    h = jnp.concatenate([h[: RANK // 2], h[RANK // 2 :]], axis=1).reshape(1, SIDE, 8, WIDE)
    sums = []
    for ref in parts:
        q = ref[FACTOR_ROWS:, :].astype(f32)
        q = q.reshape(q.shape[0] // (RANK // 2), SIDE, 8, WIDE)
        sums.append((q * h).sum(axis=1).sum(axis=1))
    sums = jnp.concatenate(sums, axis=0)
    queries = sums.shape[0]
    me = lax.axis_index("dp")
    j = lax.broadcasted_iota(jnp.int32, (queries, queries), 0)
    want = lax.broadcasted_iota(jnp.int32, (queries, queries), 1)
    last, middle = lax.shift_right_logical(j, 5), lax.shift_right_logical(j, 3)
    swap = (lax.axis_index("tensor") & 1) == 1
    y = (lax.shift_right_logical(me, 4) - jnp.where(swap, middle, last)) & 3
    x = (lax.shift_right_logical(me, 2) - jnp.where(swap, last, middle)) & 3
    step = lax.shift_right_logical(j, 1) & 3
    z = (me & 3) ^ step ^ lax.shift_right_logical(step, 1)
    source = y * 32 + x * 8 + z * 2 + (j & 1)
    place = jnp.where(source == want, 1.0, 0.0).astype(f32)
    by_row = sums.sum(axis=1, keepdims=True) * (1.0 / (RANK * RANK))
    row = (place * by_row).sum(axis=0, keepdims=True)
    out_ref[...] = jnp.where(lax.axis_index("tensor") == 3, 0.0, row)


def score(count, cross, parts):
    inside = pl.BlockSpec(memory_space=pltpu.VMEM)
    total = sum(p.shape[0] - FACTOR_ROWS for p in parts) // (RANK // 2)
    return pl.pallas_call(
        lambda *refs: score_kernel(count, *refs),
        out_shape=jax.ShapeDtypeStruct((1, total), jnp.float32),
        in_specs=[inside] * (1 + SIDE),
        out_specs=inside,
        compiler_params=pltpu.CompilerParams(vmem_limit_bytes=SMALL_VMEM),
        name="score",
    )(cross, *parts)


def ring(names, step, size):
    def to(i, t):
        stride = RINGS[names[t & 1]]
        at = (i // stride) % SIDE
        return (i + ((at + step) % SIDE - at) * stride) * 4 + t

    return [(i * 4 + t, to(i, t)) for i in range(size) for t in range(4)]


def flipped(stride, mask, size):
    def to(i):
        at = (i // stride) % SIDE
        return i + ((at ^ mask) - at) * stride

    return [(i, to(i)) for i in range(size)]


def body(
    layer_inputs, gate_pre, up_pre, hidden_grad, output_grad,
    proj_in, proj_out, proj_gate, proj_up, proj_hidden, query_grads,
):
    size = lax.axis_size("dp")

    def around(value, names):
        far, near, back = [lax.ppermute(value, ("dp", "tensor"), ring(names, s, size)) for s in (2, 1, 3)]
        return [value, near, far, back]

    def crossed(value, mask):
        return lax.ppermute(value, "tensor", [(i, i ^ mask) for i in range(4)])

    def shifted(value, step):
        return lax.ppermute(value, "tensor", [(i, (i + step) % 4) for i in range(4)])

    stay = lambda v: pltpu.with_memory_space_constraint(v, pltpu.HBM)
    gate_pre, up_pre, hidden_grad, layer_inputs, output_grad = map(stay, (gate_pre, up_pre, hidden_grad, layer_inputs, output_grad))
    own, other, pieces = project(
        gate_pre, up_pre, hidden_grad, layer_inputs, output_grad,
        proj_in, proj_out, proj_gate, proj_up, proj_hidden, query_grads,
    )
    keep, send = chip_sums(own, crossed(other, 1))
    message, cross = gram((keep, crossed(send, 2)), pieces)
    for mask in (1, 3):
        message = merge([message, lax.ppermute(message, "dp", flipped(RINGS["z"], mask, size))])
    message = merge(around(message, "xy"))
    part = score(layer_inputs.shape[0] * size, cross, around(message, "yx"))
    parts = [part] + [shifted(part, s) for s in (1, 2, 3)]
    at = lax.axis_index("tensor")

    def of(index):
        picked = parts[3]
        for s in (2, 1, 0):
            picked = jnp.where((at - index) % 4 == s, parts[s], picked)
        return picked

    return ((of(0) + of(1)) + of(2)).reshape(-1, 1)


def solution(mesh):
    placed = (
        P("dp", "tensor"), P("dp", "tensor"), P("dp", "tensor"), P("dp", "tensor"), P("dp", "tensor"),
        P(), P(), P("tensor", None), P("tensor", None), P("tensor", None),
        P("dp", None, None, None),
    )
    return jax.shard_map(body, mesh=mesh, in_specs=placed, out_specs=P(None, "dp"), check_vma=False)
```

```python
import jax
import jax.numpy as jnp
from jax import lax
from jax.experimental import pallas as pl
from jax.experimental.pallas import tpu as pltpu
from jax.sharding import PartitionSpec as P

HIGH = lax.Precision.HIGHEST
DAMP = 0.1
RANK = 64
WIDE = 2 * RANK
STRIP = 128
AHEAD = 3
SIDE = 4
VMEM_BYTES = 32 * 1024 * 1024

TERMS = 3
PACKED = RANK // 2 + 16
FACTOR_ROWS = TERMS * PACKED
SMALL_VMEM = 32 * 1024 * 1024
RINGS = {"y": 16, "x": 4, "z": 1}


def layer_of(tensor_at):
    return jnp.minimum(tensor_at, 2)


def rows_dot(a, b):
    return lax.dot_general(a, b, (((1,), (1,)), ((), ())), preferred_element_type=jnp.float32)


def project_kernel(
    gate_hbm, up_hbm, grad_hbm, inputs_hbm, outg_hbm,
    win_hbm, wout_hbm, wgate_hbm, wup_hbm, whid_hbm, query_hbm,
    own_ref, core_ref, pieces_ref,
    hidden_buf, side_buf, hidden_w, side_w, query_buf, sums, sems, side_sems,
):
    tensor_at = lax.axis_index("tensor")
    tokens, hidden = gate_hbm.shape
    features = inputs_hbm.shape[1]
    strips = tokens // STRIP

    def weight_copies():
        mine = pl.ds(pl.multiple_of(tensor_at * features, features), features)
        return [
            pltpu.make_async_copy(src.at[:, mine], side_w.at[i], side_sems.at[2 + i])
            for i, src in enumerate((win_hbm, wout_hbm))
        ] + [
            pltpu.make_async_copy(src, hidden_w.at[i], side_sems.at[5 + i])
            for i, src in enumerate((wgate_hbm, wup_hbm, whid_hbm))
        ]

    def chunk_copies(c):
        rows = pl.ds(pl.multiple_of(c * STRIP, STRIP), STRIP)
        return [
            pltpu.make_async_copy(src.at[rows, :], hidden_buf.at[i, rows, :], sems.at[i, c])
            for i, src in enumerate((gate_hbm, up_hbm, grad_hbm))
        ] + [
            pltpu.make_async_copy(src.at[rows, :], side_buf.at[i, rows, :], sems.at[3 + i, c])
            for i, src in enumerate((inputs_hbm, outg_hbm))
        ]

    def start(copies):
        for copy in copies:
            copy.start()

    def arrive(copies):
        for copy in copies:
            copy.wait()

    query_copy = pltpu.make_async_copy(query_hbm, query_buf, side_sems.at[4])
    query_copy.start()
    start(weight_copies())
    start(chunk_copies(0))

    @pl.loop(0, strips)
    def _(c):
        arrive(chunk_copies(c))

        @pl.when(c == 0)
        def _():
            for k in range(1, 3):
                start(chunk_copies(k))
            arrive(weight_copies())

        @pl.when((c > 0) & (c + 2 < strips))
        def _():
            start(chunk_copies(c + 2))

        at = pl.ds(pl.multiple_of(c * STRIP, STRIP), STRIP)
        g = hidden_buf[0, at, :].astype(jnp.float32)
        u = hidden_buf[1, at, :].astype(jnp.float32)
        e = hidden_buf[2, at, :].astype(jnp.float32)
        th = jnp.tanh(0.5 * g)
        p, q = 1.0 + th, 1.0 - th
        a = g * p
        gate_grad = ((e * u) * (p * (2.0 + g * q))).astype(jnp.bfloat16)
        up_grad = (e * a).astype(jnp.bfloat16)
        hid = (a * u).astype(jnp.bfloat16)
        for i, act in enumerate((gate_grad, up_grad, hid)):
            sums[i, at, :RANK] = rows_dot(act, hidden_w[i]) * (0.25 if i == 0 else 0.5)
        for i in range(2):
            sums[2 * i, at, RANK:] = rows_dot(side_buf[i, at, :], side_w[i])

    query_copy.wait()
    layer = layer_of(tensor_at)
    for q in range(2):
        rows = query_buf[q, layer].astype(jnp.float32)
        rows = jnp.where(layer == 2, rows.T, rows)
        packed = jnp.concatenate([rows[: RANK // 2], rows[RANK // 2 :]], axis=1)
        pieces_ref[q * (RANK // 2) : (q + 1) * (RANK // 2), :] = packed.astype(jnp.bfloat16)

    sums[1, :, RANK:] = sums[0, :, RANK:]
    core = tensor_at & 1
    core_ref[:tokens, :] = sums[1 - core].astype(jnp.bfloat16)
    core_ref[tokens:, :] = sums[2].astype(jnp.bfloat16)
    own_ref[:tokens, :] = sums[core]
    own_ref[tokens:, :] = sums[2]


def project(gate_pre, up_pre, hidden_grad, layer_inputs, output_grad, proj_in, proj_out, proj_gate, proj_up, proj_hidden, query_grads):
    tokens, hidden = gate_pre.shape
    features = layer_inputs.shape[1]
    inside = pl.BlockSpec(memory_space=pltpu.VMEM)
    buf = lambda *shape: pltpu.VMEM(shape, jnp.bfloat16)
    flops = 2 * tokens * (3 * hidden + 2 * features) * RANK
    return pl.pallas_call(
        project_kernel,
        out_shape=[
            jax.ShapeDtypeStruct((2 * tokens, WIDE), jnp.float32),
            jax.ShapeDtypeStruct((2 * tokens, WIDE), jnp.bfloat16),
            jax.ShapeDtypeStruct((RANK, WIDE), jnp.bfloat16),
        ],
        in_specs=[pl.BlockSpec(memory_space=pltpu.HBM)] * 11,
        out_specs=[inside] * 3,
        scratch_shapes=[
            buf(3, tokens, hidden),
            buf(2, tokens, features),
            buf(3, RANK, hidden),
            buf(2, RANK, features),
            buf(*query_grads.shape),
            pltpu.VMEM((3, tokens, WIDE), jnp.float32),
            pltpu.SemaphoreType.DMA((5, tokens // STRIP)),
            pltpu.SemaphoreType.DMA((8,)),
        ],
        compiler_params=pltpu.CompilerParams(vmem_limit_bytes=VMEM_BYTES),
        cost_estimate=pl.CostEstimate(flops=flops, bytes_accessed=17_000_000, transcendentals=tokens * hidden),
        name="project",
    )(gate_pre, up_pre, hidden_grad, layer_inputs, output_grad, *[pltpu.with_memory_space_constraint(v, pltpu.HBM) for v in (proj_in.T, proj_out.T, proj_gate.T, proj_up.T, proj_hidden.T, query_grads)])


def square_iota(axis):
    return lax.broadcasted_iota(jnp.int32, (RANK, RANK), axis)


def pack(a, b):
    row, col = square_iota(0), square_iota(1)
    both = jnp.where(row >= col, a, b)
    diag = jnp.where(row == col, b, 0.0).sum(axis=0, keepdims=True)
    diag = jnp.broadcast_to(jnp.concatenate([diag, diag], axis=1), (PACKED - RANK // 2, WIDE))
    return jnp.concatenate([jnp.concatenate([both[: RANK // 2], both[RANK // 2 :]], axis=1), diag], axis=0)


def unpack(packed):
    row, col = square_iota(0), square_iota(1)
    half = packed[: RANK // 2]
    both = jnp.concatenate([half[:, :RANK], half[:, RANK:]], axis=0)
    diag = packed[RANK // 2 : RANK // 2 + 1, :RANK]
    a = jnp.where(row >= col, both, both.T)
    b = jnp.where(row < col, both, jnp.where(row == col, diag, both.T))
    return jnp.concatenate([a, b], axis=1)


def put_sum(out_ref, value):
    for i in range(TERMS):
        term = value.astype(jnp.bfloat16)
        out_ref[i * PACKED : (i + 1) * PACKED, :] = term
        value = value - term.astype(jnp.float32)


def get_sum(ref):
    terms = [ref[i * PACKED : (i + 1) * PACKED, :].astype(jnp.float32) for i in range(TERMS)]
    return (terms[2] + terms[1]) + terms[0]


def total_of(refs):
    parts = [get_sum(ref) for ref in refs]
    while len(parts) > 1:
        parts = [a + b for a, b in zip(parts[::2], parts[1::2])]
    return parts[0]


def chip_kernel(own_ref, core_ref, keep_ref, send_ref):
    tokens = keep_ref.shape[0]
    far = lax.shift_right_logical(lax.axis_index("tensor"), 1)
    kept, sent = [pl.ds(pl.multiple_of(at * tokens, tokens), tokens) for at in (far, 1 - far)]
    keep_ref[...] = own_ref[kept, :] + core_ref[kept, :].astype(jnp.float32)
    send_ref[...] = (own_ref[sent, :] + core_ref[sent, :].astype(jnp.float32)).astype(jnp.bfloat16)


def chip_sums(own, core):
    inside = pl.BlockSpec(memory_space=pltpu.VMEM)
    shape = (own.shape[0] // 2, own.shape[1])
    return pl.pallas_call(
        chip_kernel,
        out_shape=[jax.ShapeDtypeStruct(shape, jnp.float32), jax.ShapeDtypeStruct(shape, jnp.bfloat16)],
        in_specs=[inside] * 2,
        out_specs=[inside] * 2,
        compiler_params=pltpu.CompilerParams(vmem_limit_bytes=SMALL_VMEM),
        name="chip_sums",
    )(own, core)


def gram_kernel(keep_ref, got_ref, pieces_ref, message_ref, cross_ref):
    f32 = jnp.float32
    v = keep_ref[...] + got_ref[...].astype(f32)
    m = lax.dot_general(v, v, (((0,), (0,)), ((), ())), precision=HIGH, preferred_element_type=f32)
    left = lax.broadcasted_iota(jnp.int32, (RANK, WIDE), 1) < RANK
    put_sum(message_ref, pack(m[:RANK, :RANK], m[RANK:, RANK:]))
    message_ref[FACTOR_ROWS:, :] = pieces_ref[...]
    cross_ref[...] = jnp.where(left, m[RANK:], m[:RANK])


def gram(parts, pieces):
    inside = pl.BlockSpec(memory_space=pltpu.VMEM)
    return pl.pallas_call(
        gram_kernel,
        out_shape=[
            jax.ShapeDtypeStruct((FACTOR_ROWS + pieces.shape[0], WIDE), jnp.bfloat16),
            jax.ShapeDtypeStruct((RANK, WIDE), jnp.float32),
        ],
        in_specs=[inside] * 3,
        out_specs=[inside] * 2,
        compiler_params=pltpu.CompilerParams(vmem_limit_bytes=SMALL_VMEM),
        name="gram",
    )(*parts, pieces)


def merge_kernel(*refs):
    parts, out_ref = refs[:-1], refs[-1]
    put_sum(out_ref, total_of(parts))
    rows = parts[0].shape[0] - FACTOR_ROWS
    for i, ref in enumerate(parts):
        out_ref[FACTOR_ROWS + i * rows : FACTOR_ROWS + (i + 1) * rows, :] = ref[FACTOR_ROWS:, :]


def merge(parts):
    inside = pl.BlockSpec(memory_space=pltpu.VMEM)
    rows = FACTOR_ROWS + len(parts) * (parts[0].shape[0] - FACTOR_ROWS)
    return pl.pallas_call(
        merge_kernel,
        out_shape=jax.ShapeDtypeStruct((rows, WIDE), jnp.bfloat16),
        in_specs=[inside] * len(parts),
        out_specs=inside,
        compiler_params=pltpu.CompilerParams(vmem_limit_bytes=SMALL_VMEM),
        name="merge",
    )(*parts)


def solve_two(m, rows):
    (a, b), (c, d) = m
    scale = 1.0 / (a * d - b * c)
    a, b, c, d = d * scale, b * scale, c * scale, a * scale
    return a * rows[0] - b * rows[1], d * rows[1] - c * rows[0]


def invert_pair(w):
    lane = lax.broadcasted_iota(jnp.int32, (RANK, WIDE), 1)
    row_at = lax.broadcasted_iota(jnp.int32, (RANK, WIDE), 0)
    left = lane < RANK
    column_at = jnp.where(left, lane, lane - RANK)

    def column(k):
        return jnp.where(
            left,
            jnp.broadcast_to(w[:, k : k + 1], (RANK, WIDE)),
            jnp.broadcast_to(w[:, RANK + k : RANK + k + 1], (RANK, WIDE)),
        )

    for k in range(0, RANK, 4):
        cols = [column(k + i) for i in range(4)]
        m = [[c[k + i : k + i + 1] for c in cols] for i in range(4)]
        at = column_at[:1]
        rows = [
            jnp.where((at >= k) & (at < k + 4), jnp.where(at == k + i, 1.0, 0.0), w[k + i : k + i + 1])
            for i in range(4)
        ]
        upper = [m[0][:2], m[1][:2]]
        x0, x1 = solve_two(upper, rows[:2])
        e02, e12 = solve_two(upper, (m[0][2], m[1][2]))
        e03, e13 = solve_two(upper, (m[0][3], m[1][3]))
        rest = [[m[i][2] - m[i][0] * e02 - m[i][1] * e12, m[i][3] - m[i][0] * e03 - m[i][1] * e13] for i in (2, 3)]
        n2, n3 = solve_two(rest, [rows[i] - m[i][0] * x0 - m[i][1] * x1 for i in (2, 3)])
        new = [x0 - e02 * n2 - e03 * n3, x1 - e12 * n2 - e13 * n3, n2, n3]
        out = jnp.where((column_at >= k) & (column_at < k + 4), 0.0, w)
        out = (out - cols[0] * new[0] - cols[1] * new[1]) - (cols[2] * new[2] + cols[3] * new[3])
        for i in range(4):
            out = jnp.where(row_at == k + i, new[i], out)
        w = out
    return w


def score_kernel(count, cross_ref, *refs):
    parts, out_ref = refs[:-1], refs[-1]
    f32 = jnp.float32
    lane = lax.broadcasted_iota(jnp.int32, (RANK, WIDE), 1)
    row_at = lax.broadcasted_iota(jnp.int32, (RANK, WIDE), 0)
    diag = (lane == row_at) | (lane == row_at + RANK)
    inv = invert_pair(unpack(total_of(parts)) * (1.0 / count) + jnp.where(diag, DAMP, 0.0))
    dot = lambda a, b: jnp.dot(a, b, precision=HIGH, preferred_element_type=f32)
    h = dot(dot(inv[:, :RANK], cross_ref[:, RANK:]), inv[:, RANK:])
    h = jnp.concatenate([h[: RANK // 2], h[RANK // 2 :]], axis=1).reshape(1, SIDE, 8, WIDE)
    sums = []
    for ref in parts:
        q = ref[FACTOR_ROWS:, :].astype(f32)
        q = q.reshape(q.shape[0] // (RANK // 2), SIDE, 8, WIDE)
        sums.append((q * h).sum(axis=1).sum(axis=1))
    sums = jnp.concatenate(sums, axis=0)
    queries = sums.shape[0]
    me = lax.axis_index("dp")
    j = lax.broadcasted_iota(jnp.int32, (queries, queries), 0)
    want = lax.broadcasted_iota(jnp.int32, (queries, queries), 1)
    last, middle = lax.shift_right_logical(j, 5), lax.shift_right_logical(j, 3)
    swap = (lax.axis_index("tensor") & 1) == 1
    y = (lax.shift_right_logical(me, 4) - jnp.where(swap, middle, last)) & 3
    x = (lax.shift_right_logical(me, 2) - jnp.where(swap, last, middle)) & 3
    step = lax.shift_right_logical(j, 1) & 3
    z = (me & 3) ^ step ^ lax.shift_right_logical(step, 1)
    source = y * 32 + x * 8 + z * 2 + (j & 1)
    place = jnp.where(source == want, 1.0, 0.0).astype(f32)
    by_row = sums.sum(axis=1, keepdims=True) * (1.0 / (RANK * RANK))
    row = (place * by_row).sum(axis=0, keepdims=True)
    out_ref[...] = jnp.where(lax.axis_index("tensor") == 3, 0.0, row)


def score(count, cross, parts):
    inside = pl.BlockSpec(memory_space=pltpu.VMEM)
    total = sum(p.shape[0] - FACTOR_ROWS for p in parts) // (RANK // 2)
    return pl.pallas_call(
        lambda *refs: score_kernel(count, *refs),
        out_shape=jax.ShapeDtypeStruct((1, total), jnp.float32),
        in_specs=[inside] * (1 + SIDE),
        out_specs=inside,
        compiler_params=pltpu.CompilerParams(vmem_limit_bytes=SMALL_VMEM),
        name="score",
    )(cross, *parts)


def ring(names, step, size):
    def to(i, t):
        stride = RINGS[names[t & 1]]
        at = (i // stride) % SIDE
        return (i + ((at + step) % SIDE - at) * stride) * 4 + t

    return [(i * 4 + t, to(i, t)) for i in range(size) for t in range(4)]


def flipped(stride, mask, size):
    def to(i):
        at = (i // stride) % SIDE
        return i + ((at ^ mask) - at) * stride

    return [(i, to(i)) for i in range(size)]


def body(
    layer_inputs, gate_pre, up_pre, hidden_grad, output_grad,
    proj_in, proj_out, proj_gate, proj_up, proj_hidden, query_grads,
):
    size = lax.axis_size("dp")

    def around(value, names):
        far, near, back = [lax.ppermute(value, ("dp", "tensor"), ring(names, s, size)) for s in (2, 1, 3)]
        return [value, near, far, back]

    def crossed(value, mask):
        return lax.ppermute(value, "tensor", [(i, i ^ mask) for i in range(4)])

    def shifted(value, step):
        return lax.ppermute(value, "tensor", [(i, (i + step) % 4) for i in range(4)])

    stay = lambda v: pltpu.with_memory_space_constraint(v, pltpu.HBM)
    gate_pre, up_pre, hidden_grad, layer_inputs, output_grad = map(stay, (gate_pre, up_pre, hidden_grad, layer_inputs, output_grad))
    own, other, pieces = project(
        gate_pre, up_pre, hidden_grad, layer_inputs, output_grad,
        proj_in, proj_out, proj_gate, proj_up, proj_hidden, query_grads,
    )
    keep, send = chip_sums(own, crossed(other, 1))
    message, cross = gram((keep, crossed(send, 2)), pieces)
    for mask in (1, 3):
        message = merge([message, lax.ppermute(message, "dp", flipped(RINGS["z"], mask, size))])
    message = merge(around(message, "xy"))
    part = score(layer_inputs.shape[0] * size, cross, around(message, "yx"))
    parts = [part] + [shifted(part, s) for s in (1, 2, 3)]
    at = lax.axis_index("tensor")

    def of(index):
        picked = parts[3]
        for s in (2, 1, 0):
            picked = jnp.where((at - index) % 4 == s, parts[s], picked)
        return picked

    return ((of(0) + of(1)) + of(2)).reshape(-1, 1)


def solution(mesh):
    placed = (
        P("dp", "tensor"), P("dp", "tensor"), P("dp", "tensor"), P("dp", "tensor"), P("dp", "tensor"),
        P(), P(), P("tensor", None), P("tensor", None), P("tensor", None),
        P("dp", None, None, None),
    )
    return jax.shard_map(body, mesh=mesh, in_specs=placed, out_specs=P(None, "dp"), check_vma=False)
```

```python
import jax
import jax.numpy as jnp
from jax import lax
from jax.experimental import pallas as pl
from jax.experimental.pallas import tpu as pltpu
from jax.sharding import PartitionSpec as P

HIGH = lax.Precision.HIGHEST
DAMP = 0.1
RANK = 64
WIDE = 2 * RANK
STRIP = 128
AHEAD = 3
SIDE = 4
VMEM_BYTES = 32 * 1024 * 1024

TERMS = 3
PACKED = RANK // 2 + 16
FACTOR_ROWS = TERMS * PACKED
SMALL_VMEM = 32 * 1024 * 1024
RINGS = {"y": 16, "x": 4, "z": 1}


def layer_of(tensor_at):
    return jnp.minimum(tensor_at, 2)


def rows_dot(a, b):
    return lax.dot_general(a, b, (((1,), (1,)), ((), ())), preferred_element_type=jnp.float32)


def project_kernel(
    gate_hbm, up_hbm, grad_hbm, inputs_hbm, outg_hbm,
    win_hbm, wout_hbm, wgate_hbm, wup_hbm, whid_hbm, query_hbm,
    own_ref, core_ref, pieces_ref,
    hidden_buf, side_buf, hidden_w, side_w, query_buf, sums, sems, side_sems,
):
    tensor_at = lax.axis_index("tensor")
    tokens, hidden = gate_hbm.shape
    features = inputs_hbm.shape[1]
    strips = tokens // STRIP

    def weight_copies():
        mine = pl.ds(pl.multiple_of(tensor_at * features, features), features)
        return [
            pltpu.make_async_copy(src.at[:, mine], side_w.at[i], side_sems.at[2 + i])
            for i, src in enumerate((win_hbm, wout_hbm))
        ] + [
            pltpu.make_async_copy(src, hidden_w.at[i], side_sems.at[5 + i])
            for i, src in enumerate((wgate_hbm, wup_hbm, whid_hbm))
        ]

    def chunk_copies(c):
        rows = pl.ds(pl.multiple_of(c * STRIP, STRIP), STRIP)
        return [
            pltpu.make_async_copy(src.at[rows, :], hidden_buf.at[i, rows, :], sems.at[i, c])
            for i, src in enumerate((gate_hbm, up_hbm, grad_hbm))
        ] + [
            pltpu.make_async_copy(src.at[rows, :], side_buf.at[i, rows, :], sems.at[3 + i, c])
            for i, src in enumerate((inputs_hbm, outg_hbm))
        ]

    def start(copies):
        for copy in copies:
            copy.start()

    def arrive(copies):
        for copy in copies:
            copy.wait()

    query_copy = pltpu.make_async_copy(query_hbm, query_buf, side_sems.at[4])
    query_copy.start()
    start(weight_copies())
    start(chunk_copies(0))

    @pl.loop(0, strips)
    def _(c):
        arrive(chunk_copies(c))

        @pl.when(c == 0)
        def _():
            for k in range(1, strips):
                start(chunk_copies(k))
            arrive(weight_copies())

        at = pl.ds(pl.multiple_of(c * STRIP, STRIP), STRIP)
        g = hidden_buf[0, at, :].astype(jnp.float32)
        u = hidden_buf[1, at, :].astype(jnp.float32)
        e = hidden_buf[2, at, :].astype(jnp.float32)
        half = 0.5 * g
        th = jnp.tanh(half)
        p = 1.0 + th
        a = half * p
        gate_grad = ((e * u) * (p * (1.0 + (g - a)))).astype(jnp.bfloat16)
        up_grad = (e * a).astype(jnp.bfloat16)
        hid = (a * u).astype(jnp.bfloat16)
        for i, act in enumerate((gate_grad, up_grad, hid)):
            sums[i, at, :RANK] = rows_dot(act, hidden_w[i]) * (0.5 if i == 0 else 1.0)
        for i in range(2):
            sums[2 * i, at, RANK:] = rows_dot(side_buf[i, at, :], side_w[i])

    query_copy.wait()
    layer = layer_of(tensor_at)
    for q in range(2):
        rows = query_buf[q, layer].astype(jnp.float32)
        rows = jnp.where(layer == 2, rows.T, rows)
        packed = jnp.concatenate([rows[: RANK // 2], rows[RANK // 2 :]], axis=1)
        pieces_ref[q * (RANK // 2) : (q + 1) * (RANK // 2), :] = packed.astype(jnp.bfloat16)

    sums[1, :, RANK:] = sums[0, :, RANK:]
    core = tensor_at & 1
    core_ref[:tokens, :] = sums[1 - core].astype(jnp.bfloat16)
    core_ref[tokens:, :] = sums[2].astype(jnp.bfloat16)
    own_ref[:tokens, :] = sums[core]
    own_ref[tokens:, :] = sums[2]


def project(gate_pre, up_pre, hidden_grad, layer_inputs, output_grad, proj_in, proj_out, proj_gate, proj_up, proj_hidden, query_grads):
    tokens, hidden = gate_pre.shape
    features = layer_inputs.shape[1]
    inside = pl.BlockSpec(memory_space=pltpu.VMEM)
    buf = lambda *shape: pltpu.VMEM(shape, jnp.bfloat16)
    flops = 2 * tokens * (3 * hidden + 2 * features) * RANK
    return pl.pallas_call(
        project_kernel,
        out_shape=[
            jax.ShapeDtypeStruct((2 * tokens, WIDE), jnp.float32),
            jax.ShapeDtypeStruct((2 * tokens, WIDE), jnp.bfloat16),
            jax.ShapeDtypeStruct((RANK, WIDE), jnp.bfloat16),
        ],
        in_specs=[pl.BlockSpec(memory_space=pltpu.HBM)] * 11,
        out_specs=[inside] * 3,
        scratch_shapes=[
            buf(3, tokens, hidden),
            buf(2, tokens, features),
            buf(3, RANK, hidden),
            buf(2, RANK, features),
            buf(*query_grads.shape),
            pltpu.VMEM((3, tokens, WIDE), jnp.float32),
            pltpu.SemaphoreType.DMA((5, tokens // STRIP)),
            pltpu.SemaphoreType.DMA((8,)),
        ],
        compiler_params=pltpu.CompilerParams(vmem_limit_bytes=VMEM_BYTES),
        cost_estimate=pl.CostEstimate(flops=flops, bytes_accessed=17_000_000, transcendentals=tokens * hidden),
        name="project",
    )(gate_pre, up_pre, hidden_grad, layer_inputs, output_grad, *[pltpu.with_memory_space_constraint(v, pltpu.HBM) for v in (proj_in.T, proj_out.T, proj_gate.T, proj_up.T, proj_hidden.T, query_grads)])


def square_iota(axis):
    return lax.broadcasted_iota(jnp.int32, (RANK, RANK), axis)


def pack(a, b):
    row, col = square_iota(0), square_iota(1)
    both = jnp.where(row >= col, a, b)
    diag = jnp.where(row == col, b, 0.0).sum(axis=0, keepdims=True)
    diag = jnp.broadcast_to(jnp.concatenate([diag, diag], axis=1), (PACKED - RANK // 2, WIDE))
    return jnp.concatenate([jnp.concatenate([both[: RANK // 2], both[RANK // 2 :]], axis=1), diag], axis=0)


def unpack(packed):
    row, col = square_iota(0), square_iota(1)
    half = packed[: RANK // 2]
    both = jnp.concatenate([half[:, :RANK], half[:, RANK:]], axis=0)
    diag = packed[RANK // 2 : RANK // 2 + 1, :RANK]
    a = jnp.where(row >= col, both, both.T)
    b = jnp.where(row < col, both, jnp.where(row == col, diag, both.T))
    return jnp.concatenate([a, b], axis=1)


def put_sum(out_ref, value):
    for i in range(TERMS):
        term = value.astype(jnp.bfloat16)
        out_ref[i * PACKED : (i + 1) * PACKED, :] = term
        value = value - term.astype(jnp.float32)


def get_sum(ref):
    terms = [ref[i * PACKED : (i + 1) * PACKED, :].astype(jnp.float32) for i in range(TERMS)]
    return (terms[2] + terms[1]) + terms[0]


def total_of(refs):
    parts = [get_sum(ref) for ref in refs]
    while len(parts) > 1:
        parts = [a + b for a, b in zip(parts[::2], parts[1::2])]
    return parts[0]


def chip_kernel(own_ref, core_ref, keep_ref, send_ref):
    tokens = keep_ref.shape[0]
    far = lax.shift_right_logical(lax.axis_index("tensor"), 1)
    kept, sent = [pl.ds(pl.multiple_of(at * tokens, tokens), tokens) for at in (far, 1 - far)]
    keep_ref[...] = own_ref[kept, :] + core_ref[kept, :].astype(jnp.float32)
    send_ref[...] = (own_ref[sent, :] + core_ref[sent, :].astype(jnp.float32)).astype(jnp.bfloat16)


def chip_sums(own, core):
    inside = pl.BlockSpec(memory_space=pltpu.VMEM)
    shape = (own.shape[0] // 2, own.shape[1])
    return pl.pallas_call(
        chip_kernel,
        out_shape=[jax.ShapeDtypeStruct(shape, jnp.float32), jax.ShapeDtypeStruct(shape, jnp.bfloat16)],
        in_specs=[inside] * 2,
        out_specs=[inside] * 2,
        compiler_params=pltpu.CompilerParams(vmem_limit_bytes=SMALL_VMEM),
        name="chip_sums",
    )(own, core)


def gram_kernel(keep_ref, got_ref, pieces_ref, message_ref, cross_ref):
    f32 = jnp.float32
    v = keep_ref[...] + got_ref[...].astype(f32)
    m = lax.dot_general(v, v, (((0,), (0,)), ((), ())), precision=HIGH, preferred_element_type=f32)
    left = lax.broadcasted_iota(jnp.int32, (RANK, WIDE), 1) < RANK
    put_sum(message_ref, pack(m[:RANK, :RANK], m[RANK:, RANK:]))
    message_ref[FACTOR_ROWS:, :] = pieces_ref[...]
    cross_ref[...] = jnp.where(left, m[RANK:], m[:RANK])


def gram(parts, pieces):
    inside = pl.BlockSpec(memory_space=pltpu.VMEM)
    return pl.pallas_call(
        gram_kernel,
        out_shape=[
            jax.ShapeDtypeStruct((FACTOR_ROWS + pieces.shape[0], WIDE), jnp.bfloat16),
            jax.ShapeDtypeStruct((RANK, WIDE), jnp.float32),
        ],
        in_specs=[inside] * 3,
        out_specs=[inside] * 2,
        compiler_params=pltpu.CompilerParams(vmem_limit_bytes=SMALL_VMEM),
        name="gram",
    )(*parts, pieces)


def merge_kernel(*refs):
    parts, out_ref = refs[:-1], refs[-1]
    put_sum(out_ref, total_of(parts))
    rows = parts[0].shape[0] - FACTOR_ROWS
    for i, ref in enumerate(parts):
        out_ref[FACTOR_ROWS + i * rows : FACTOR_ROWS + (i + 1) * rows, :] = ref[FACTOR_ROWS:, :]


def merge(parts):
    inside = pl.BlockSpec(memory_space=pltpu.VMEM)
    rows = FACTOR_ROWS + len(parts) * (parts[0].shape[0] - FACTOR_ROWS)
    return pl.pallas_call(
        merge_kernel,
        out_shape=jax.ShapeDtypeStruct((rows, WIDE), jnp.bfloat16),
        in_specs=[inside] * len(parts),
        out_specs=inside,
        compiler_params=pltpu.CompilerParams(vmem_limit_bytes=SMALL_VMEM),
        name="merge",
    )(*parts)


def solve_two(m, rows):
    (a, b), (c, d) = m
    scale = 1.0 / (a * d - b * c)
    a, b, c, d = d * scale, b * scale, c * scale, a * scale
    return a * rows[0] - b * rows[1], d * rows[1] - c * rows[0]


def invert_pair(w):
    lane = lax.broadcasted_iota(jnp.int32, (RANK, WIDE), 1)
    row_at = lax.broadcasted_iota(jnp.int32, (RANK, WIDE), 0)
    left = lane < RANK
    column_at = jnp.where(left, lane, lane - RANK)

    def column(k):
        return jnp.where(
            left,
            jnp.broadcast_to(w[:, k : k + 1], (RANK, WIDE)),
            jnp.broadcast_to(w[:, RANK + k : RANK + k + 1], (RANK, WIDE)),
        )

    for k in range(0, RANK, 4):
        cols = [column(k + i) for i in range(4)]
        m = [[c[k + i : k + i + 1] for c in cols] for i in range(4)]
        at = column_at[:1]
        rows = [
            jnp.where((at >= k) & (at < k + 4), jnp.where(at == k + i, 1.0, 0.0), w[k + i : k + i + 1])
            for i in range(4)
        ]
        upper = [m[0][:2], m[1][:2]]
        x0, x1 = solve_two(upper, rows[:2])
        e02, e12 = solve_two(upper, (m[0][2], m[1][2]))
        e03, e13 = solve_two(upper, (m[0][3], m[1][3]))
        rest = [[m[i][2] - m[i][0] * e02 - m[i][1] * e12, m[i][3] - m[i][0] * e03 - m[i][1] * e13] for i in (2, 3)]
        n2, n3 = solve_two(rest, [rows[i] - m[i][0] * x0 - m[i][1] * x1 for i in (2, 3)])
        new = [x0 - e02 * n2 - e03 * n3, x1 - e12 * n2 - e13 * n3, n2, n3]
        out = jnp.where((column_at >= k) & (column_at < k + 4), 0.0, w)
        out = (out - cols[0] * new[0] - cols[1] * new[1]) - (cols[2] * new[2] + cols[3] * new[3])
        for i in range(4):
            out = jnp.where(row_at == k + i, new[i], out)
        w = out
    return w


def score_kernel(count, cross_ref, *refs):
    parts, out_ref = refs[:-1], refs[-1]
    f32 = jnp.float32
    lane = lax.broadcasted_iota(jnp.int32, (RANK, WIDE), 1)
    row_at = lax.broadcasted_iota(jnp.int32, (RANK, WIDE), 0)
    diag = (lane == row_at) | (lane == row_at + RANK)
    inv = invert_pair(unpack(total_of(parts)) * (1.0 / count) + jnp.where(diag, DAMP, 0.0))
    dot = lambda a, b: jnp.dot(a, b, precision=HIGH, preferred_element_type=f32)
    h = dot(dot(inv[:, :RANK], cross_ref[:, RANK:]), inv[:, RANK:])
    h = jnp.concatenate([h[: RANK // 2], h[RANK // 2 :]], axis=1).reshape(1, SIDE, 8, WIDE)
    sums = []
    for ref in parts:
        q = ref[FACTOR_ROWS:, :].astype(f32)
        q = q.reshape(q.shape[0] // (RANK // 2), SIDE, 8, WIDE)
        sums.append((q * h).sum(axis=1).sum(axis=1))
    sums = jnp.concatenate(sums, axis=0)
    queries = sums.shape[0]
    me = lax.axis_index("dp")
    j = lax.broadcasted_iota(jnp.int32, (queries, queries), 0)
    want = lax.broadcasted_iota(jnp.int32, (queries, queries), 1)
    last, middle = lax.shift_right_logical(j, 5), lax.shift_right_logical(j, 3)
    swap = (lax.axis_index("tensor") & 1) == 1
    y = (lax.shift_right_logical(me, 4) - jnp.where(swap, middle, last)) & 3
    x = (lax.shift_right_logical(me, 2) - jnp.where(swap, last, middle)) & 3
    step = lax.shift_right_logical(j, 1) & 3
    z = (me & 3) ^ step ^ lax.shift_right_logical(step, 1)
    source = y * 32 + x * 8 + z * 2 + (j & 1)
    place = jnp.where(source == want, 1.0, 0.0).astype(f32)
    by_row = sums.sum(axis=1, keepdims=True) * (1.0 / (RANK * RANK))
    row = (place * by_row).sum(axis=0, keepdims=True)
    out_ref[...] = jnp.where(lax.axis_index("tensor") == 3, 0.0, row)


def score(count, cross, parts):
    inside = pl.BlockSpec(memory_space=pltpu.VMEM)
    total = sum(p.shape[0] - FACTOR_ROWS for p in parts) // (RANK // 2)
    return pl.pallas_call(
        lambda *refs: score_kernel(count, *refs),
        out_shape=jax.ShapeDtypeStruct((1, total), jnp.float32),
        in_specs=[inside] * (1 + SIDE),
        out_specs=inside,
        compiler_params=pltpu.CompilerParams(vmem_limit_bytes=SMALL_VMEM),
        name="score",
    )(cross, *parts)


def ring(names, step, size):
    def to(i, t):
        stride = RINGS[names[t & 1]]
        at = (i // stride) % SIDE
        return (i + ((at + step) % SIDE - at) * stride) * 4 + t

    return [(i * 4 + t, to(i, t)) for i in range(size) for t in range(4)]


def flipped(stride, mask, size):
    def to(i):
        at = (i // stride) % SIDE
        return i + ((at ^ mask) - at) * stride

    return [(i, to(i)) for i in range(size)]


def body(
    layer_inputs, gate_pre, up_pre, hidden_grad, output_grad,
    proj_in, proj_out, proj_gate, proj_up, proj_hidden, query_grads,
):
    size = lax.axis_size("dp")

    def around(value, names):
        far, near, back = [lax.ppermute(value, ("dp", "tensor"), ring(names, s, size)) for s in (2, 1, 3)]
        return [value, near, far, back]

    def crossed(value, mask):
        return lax.ppermute(value, "tensor", [(i, i ^ mask) for i in range(4)])

    def shifted(value, step):
        return lax.ppermute(value, "tensor", [(i, (i + step) % 4) for i in range(4)])

    stay = lambda v: pltpu.with_memory_space_constraint(v, pltpu.HBM)
    gate_pre, up_pre, hidden_grad, layer_inputs, output_grad = map(stay, (gate_pre, up_pre, hidden_grad, layer_inputs, output_grad))
    own, other, pieces = project(
        gate_pre, up_pre, hidden_grad, layer_inputs, output_grad,
        proj_in, proj_out, proj_gate, proj_up, proj_hidden, query_grads,
    )
    keep, send = chip_sums(own, crossed(other, 1))
    message, cross = gram((keep, crossed(send, 2)), pieces)
    for mask in (1, 3):
        message = merge([message, lax.ppermute(message, "dp", flipped(RINGS["z"], mask, size))])
    message = merge(around(message, "xy"))
    part = score(layer_inputs.shape[0] * size, cross, around(message, "yx"))
    parts = [part] + [shifted(part, s) for s in (1, 2, 3)]
    at = lax.axis_index("tensor")

    def of(index):
        picked = parts[3]
        for s in (2, 1, 0):
            picked = jnp.where((at - index) % 4 == s, parts[s], picked)
        return picked

    return ((of(0) + of(1)) + of(2)).reshape(-1, 1)


def solution(mesh):
    placed = (
        P("dp", "tensor"), P("dp", "tensor"), P("dp", "tensor"), P("dp", "tensor"), P("dp", "tensor"),
        P(), P(), P("tensor", None), P("tensor", None), P("tensor", None),
        P("dp", None, None, None),
    )
    return jax.shard_map(body, mesh=mesh, in_specs=placed, out_specs=P(None, "dp"), check_vma=False)
```
